256 devices in a mesh: wide: 32 (over z, y), narrow: 8 (over x, core).
Axes of the slice: x: 4, y: 4, z: 8, core: 2. Of those that a mesh axis runs over, the one named last changes fastest.
Arguments:
- multipoles: bfloat16 [49, 128, 32, 128], P(None, 'wide', 'narrow'), may hold values from -6 to 6
- translate_far: bfloat16 [7, 7, 7, 49, 49], replicated, may hold values from -0.0625 to 0.0625
- translate_up: bfloat16 [8, 49, 49], replicated, may hold values from -0.3125 to 0.3125
Outputs:
- locals_fine: float32 [49, 128, 32, 128], P(None, 'wide', 'narrow')
- parents: bfloat16 [49, 64, 16, 64], P(None, 'wide', 'narrow')
- locals_coarse: float32 [49, 64, 16, 64], P(None, 'wide', 'narrow')
The draws below stay inside these ranges and needn't reach their ends.
All inputs are finite; a program needn't handle non-finite values.
Results may differ from the reference program's by a relative error of at most 0.001.
Values may be sent and summed in bfloat16 or wider, within the bound.
No kernel may reach another device: no remote copies, remote signals or barrier semaphores. Data moves between devices by JAX's collectives and lax.ppermute only.
A program may use at most 128 MiB of HBM per device.

```python
import jax
import jax.numpy as jnp
import numpy as np

COEF = 49
NY = 128
NX = 128
NZ = 32


def shard_levels(rng, dims, shards, low, top_value):
    loudness = 1.0
    for axis_at, shards_of in shards:
        heights = jax.random.uniform(jax.random.fold_in(jax.random.fold_in(rng, 6), axis_at), (shards_of,), jnp.float32, low / len(shards), top_value / len(shards))
        loudness = loudness * jnp.repeat(jnp.exp(heights), dims[axis_at] // shards_of).reshape((-1,) + (1,) * (len(dims) - 1 - axis_at))
    return loudness


def centred(stream_key, extent, deviation, bound, split=(), kind=jnp.bfloat16):
    array = deviation * jax.random.normal(stream_key, extent, jnp.float32)
    if split:
        array = array * shard_levels(stream_key, extent, split, -0.22, 0.18)
    return jnp.clip(array, -bound, bound).astype(kind)


def setup_inputs(seed: int = 0) -> dict:
    seeds = jax.random.split(jax.random.key(seed), 4)
    multipoles = centred(seeds[0], (COEF, NX, NZ, NY), 1.0, 6.0, ((1, 32), (2, 8)))
    translate_far = centred(seeds[1], (7, 7, 7, COEF, COEF), (189 * COEF) ** -0.5, 0.0625)
    translate_up = centred(seeds[2], (8, COEF, COEF), (8 * COEF) ** -0.5, 0.3125)
    return dict(multipoles=multipoles, translate_far=translate_far, translate_up=translate_up)


def offset_tables():
    shifts = [(sx, sz, sy) for sx in (-1, 0, 1) for sz in (-1, 0, 1) for sy in (-1, 0, 1)]
    index_x = np.zeros((27, 8, 8), np.int32)
    index_z = np.zeros((27, 8, 8), np.int32)
    index_y = np.zeros((27, 8, 8), np.int32)
    allowed = np.zeros((27, 8, 8), bool)
    for number, shift in enumerate(shifts):
        for source in range(8):
            for target in range(8):
                source_pos = (source // 4, (source // 2) % 2, source % 2)
                target_pos = (target // 4, (target // 2) % 2, target % 2)
                offset = [2 * shift[d] + source_pos[d] - target_pos[d] for d in range(3)]
                index_x[number, source, target] = offset[0] + 3
                index_z[number, source, target] = offset[1] + 3
                index_y[number, source, target] = offset[2] + 3
                allowed[number, source, target] = max(abs(v) for v in offset) > 1
    return shifts, index_x, index_z, index_y, allowed


def coupling_blocks(translate_far):
    shifts, index_x, index_z, index_y, allowed = offset_tables()
    coef = translate_far.shape[-1]
    picked = translate_far[index_x, index_z, index_y]
    picked = jnp.where(jnp.asarray(allowed)[:, :, :, None, None], picked, jnp.zeros_like(picked))
    return shifts, picked.transpose(0, 1, 3, 2, 4).reshape(27, 8 * coef, 8 * coef)


def to_blocks(field):
    coef, size_x, size_z, size_y = field.shape
    field = field.reshape(coef, size_x // 2, 2, size_z // 2, 2, size_y // 2, 2)
    field = field.transpose(2, 4, 6, 0, 1, 3, 5)
    return field.reshape(8 * coef, size_x // 2, size_z // 2, size_y // 2)


def from_blocks(blocks, coef):
    rows, par_x, par_z, par_y = blocks.shape
    blocks = blocks.reshape(2, 2, 2, coef, par_x, par_z, par_y)
    return blocks.transpose(3, 4, 0, 5, 1, 6, 2).reshape(coef, 2 * par_x, 2 * par_z, 2 * par_y)


def far_field(field, translate_far):
    shifts, coupling = coupling_blocks(translate_far)
    coef, size_x, size_z, size_y = field.shape
    padded = jnp.pad(field, ((0, 0), (2, 2), (2, 2), (2, 2)))
    blocked = to_blocks(padded).astype(jnp.float32)
    coupling = coupling.astype(jnp.float32)
    par_x, par_z, par_y = size_x // 2, size_z // 2, size_y // 2
    total = jnp.zeros((8 * coef, par_x, par_z, par_y), jnp.float32)
    for number, shift in enumerate(shifts):
        window = blocked[:, 1 + shift[0]:1 + shift[0] + par_x, 1 + shift[1]:1 + shift[1] + par_z, 1 + shift[2]:1 + shift[2] + par_y]
        total = total + jnp.einsum("ba,bxzy->axzy", coupling[number], window)
    return from_blocks(total, coef)


def reference(multipoles, translate_far, translate_up):
    coef = multipoles.shape[0]
    locals_fine = far_field(multipoles, translate_far)
    children = to_blocks(multipoles).astype(jnp.float32)
    upward = translate_up.reshape(8 * coef, coef).astype(jnp.float32)
    parents = jnp.einsum("bk,bxzy->kxzy", upward, children).astype(jnp.bfloat16)
    locals_coarse = far_field(parents, translate_far)
    return locals_fine, parents, locals_coarse
```

```python
import jax
import jax.numpy as jnp
from jax import lax
from jax.experimental import pallas as pl
from jax.experimental.pallas import tpu as pltpu
from jax.sharding import PartitionSpec as P

F32 = jnp.float32
BF16 = jnp.bfloat16
NT = (((1,), (1,)), ((), ()))
COEF = 49
SLOT = 64
NY = 128
HY = 64
FINE = 4 * NY
ROWS = FINE + 3 * HY
SEG = NY + 8
SUMS = 4 * SEG + HY
VMEM = 100 * 2**20 // 2


def dot(a, b):
    return jnp.dot(a, b, preferred_element_type=F32)


def eye(n):
    rows = lax.broadcasted_iota(jnp.int32, (n, n), 0)
    cols = lax.broadcasted_iota(jnp.int32, (n, n), 1)
    return jnp.where(rows == cols, 1.0, 0.0).astype(BF16)


def tables_kernel(far_ref, up_ref, out_ref, pairs_ref, wide_ref):
    step = pl.program_id(0)
    near = jnp.abs(step - 3) <= 1
    out_ref[...] = jnp.zeros_like(out_ref)

    def at_dy(dy, carry):
        close = jnp.logical_and(near, jnp.abs(dy - 3) <= 1)
        keep = jnp.where(close, 0.0, 1.0)
        for dz in range(7):
            block = far_ref[0, dz, dy]
            if abs(dz - 3) <= 1:
                block = (block.astype(F32) * keep).astype(BF16)
            for sz in range(3):
                for cz in range(2):
                    to = 2 * sz + 1 + cz - dz
                    if 0 <= to <= 1:
                        out_ref[dy, sz, 0, pl.ds(SLOT * cz, COEF), pl.ds(SLOT * to, COEF)] = block
        return carry

    lax.fori_loop(0, 7, at_dy, 0)

    @pl.when(step == 0)
    def _():
        wide_ref[...] = up_ref[...].astype(F32)
        pairs_ref[...] = jnp.zeros_like(pairs_ref)
        for child in range(8):
            block = wide_ref[pl.ds(child, COEF, stride=8), :].astype(BF16)
            pairs_ref[pl.ds(SLOT * (child // 2), COEF), pl.ds(SLOT * (child % 2), COEF)] = block


def make_tables(far, up):
    return pl.pallas_call(
        tables_kernel,
        grid=(7,),
        in_specs=[
            pl.BlockSpec((1, 7, 7, COEF, COEF), lambda i: (i, 0, 0, 0, 0)),
            pl.BlockSpec((8 * COEF, COEF), lambda i: (0, 0)),
        ],
        out_specs=[
            pl.BlockSpec((7, 3, 1, 128, 128), lambda i: (0, 0, i, 0, 0)),
            pl.BlockSpec((256, 128), lambda i: (0, 0)),
        ],
        out_shape=[
            jax.ShapeDtypeStruct((7, 3, 7, 128, 128), BF16),
            jax.ShapeDtypeStruct((256, 128), BF16),
        ],
        scratch_shapes=[pltpu.VMEM((8 * COEF, COEF), F32)],
        compiler_params=pltpu.CompilerParams(vmem_limit_bytes=VMEM),
        cost_estimate=pl.CostEstimate(flops=0, bytes_accessed=10_000_000, transcendentals=0),
        name="tables",
    )(far, up)


def pack_kernel(where_ref, own_ref, a_ref, b_ref, pairs_ref, out_ref, in_ref, par_ref, bricks, halves, shuffled):
    odd, core = where_ref[0], where_ref[1]
    tail = jnp.zeros((3, 16 * (SLOT - COEF), NY), F32)
    bricks[:, pl.ds(16 * COEF, 16 * (SLOT - COEF)), :] = tail
    bricks[1, pl.ds(0, 16 * COEF), :] = own_ref[...].astype(F32)
    bricks[2 - 2 * odd, pl.ds(0, 16 * COEF), :] = a_ref[...].astype(F32)
    bricks[2 * odd, pl.ds(0, 16 * COEF), :] = b_ref[...].astype(F32)
    unit = eye(NY)
    pairs = pairs_ref[...]
    low = lax.broadcasted_iota(jnp.int32, (HY, 128), 1) < SLOT
    for xq in range(6):
        for q in range(2):
            zp = q + core - 2 * q * core
            cells = []
            for cx in range(2):
                for cz in range(2):
                    first = (2 * (xq % 2) + cx) * 4 + 2 * zp + cz
                    cells.append(bricks[xq // 2, pl.ds(first, SLOT, stride=16), :].astype(BF16))
            cells = jnp.concatenate(cells, axis=0)
            turned = lax.dot_general(unit, cells, NT, preferred_element_type=F32).astype(BF16)
            if 1 <= xq <= 4:
                (out_ref if q == 0 else in_ref)[pl.ds((xq - 1) * NY, NY), :] = turned
            halves[zp] = dot(turned, pairs)
        first = halves[0, pl.ds(0, HY, stride=2), :] + pltpu.roll(halves[0, pl.ds(1, HY, stride=2), :], SLOT, 1)
        second = pltpu.roll(halves[1, pl.ds(0, HY, stride=2), :], SLOT, 1) + halves[1, pl.ds(1, HY, stride=2), :]
        parent = jnp.where(low, first, second).astype(BF16)
        for ref in (out_ref, in_ref):
            ref[pl.ds(FINE + (xq // 2) * HY, HY), pl.ds(128 * (xq % 2), 128)] = parent
        if xq // 2 == 1:
            turned = lax.dot_general(unit, parent, NT, preferred_element_type=F32)
            for z in range(2):
                shuffled[pl.ds((xq - 2) * 2 + z, COEF, stride=4), :] = turned[z * SLOT : z * SLOT + COEF]
    par_ref[...] = shuffled[...].astype(BF16)


def pack(where, own, a, b, pairs):
    vmem = pl.BlockSpec(memory_space=pltpu.VMEM)
    return pl.pallas_call(
        pack_kernel,
        in_specs=[pl.BlockSpec(memory_space=pltpu.SMEM)] + [vmem] * 4,
        out_specs=[vmem] * 3,
        out_shape=[
            jax.ShapeDtypeStruct((ROWS, 256), BF16),
            jax.ShapeDtypeStruct((ROWS, 256), BF16),
            jax.ShapeDtypeStruct((4 * COEF, HY), BF16),
        ],
        scratch_shapes=[
            pltpu.VMEM((3, 16 * SLOT, NY), F32),
            pltpu.VMEM((2, NY, 128), F32),
            pltpu.VMEM((4 * COEF, HY), F32),
        ],
        compiler_params=pltpu.CompilerParams(vmem_limit_bytes=VMEM),
        name="pack",
    )(where, own, a, b, pairs)


def operator(tables, at):
    return jnp.concatenate(
        [tables[at][1:7].reshape(6 * 128, 128), tables[at][0:6].reshape(6 * 128, 128)], axis=1
    )


def slabs(ref):
    part = [ref[pl.ds(x * NY, NY), :] for x in range(4)]
    return jnp.concatenate([jnp.concatenate(part[x : x + 3], axis=1) for x in range(2)], axis=0)


def coarse_slab(ref):
    return jnp.concatenate([ref[pl.ds(FINE + x * HY, HY), :] for x in range(3)], axis=1)


def clear_gaps(spread):
    for seg in range(5):
        spread[:, pl.ds(seg * SEG, 8), :] = jnp.zeros((7, 8, 256), F32)
    spread[:, pl.ds(8 + 4 * SEG + HY, 8), :] = jnp.zeros((7, 8, 256), F32)


def shifted(spread, seg):
    rows = NY if seg < 4 else HY
    even = lax.broadcasted_iota(jnp.int32, (rows, 256), 0) % 2 == 0
    total = None
    for dy in range(7):
        moved = spread[dy, pl.ds(5 + seg * SEG + dy, rows), :]
        if dy == 0:
            moved = jnp.where(even, 0.0, moved)
        if dy == 6:
            moved = jnp.where(even, moved, 0.0)
        total = moved if total is None else total + moved
    return total


def put(spread, fine_out, fine_in, coarse):
    for px in range(2):
        spread[pl.ds(8 + px * SEG, NY), :] = fine_out[px * NY : (px + 1) * NY]
        spread[pl.ds(8 + (2 + px) * SEG, NY), :] = fine_in[px * NY : (px + 1) * NY]
    spread[pl.ds(8 + 4 * SEG, HY), :] = coarse


def inner_kernel(where_ref, out_ref, in_ref, tables_ref, sums_ref, tables, spread, sems):
    sign = 1 - 2 * where_ref[1]

    def fetch(dy):
        return pltpu.make_async_copy(tables_ref.at[dy], tables.at[dy], sems.at[dy])

    for dy in range(7):
        fetch(dy).start()
    clear_gaps(spread)

    def at_dy(dy, carry):
        fetch(dy).wait()
        here = tables.at[dy]
        of_out, of_in = slabs(out_ref), slabs(in_ref)
        same = dot(jnp.concatenate([of_out, of_in, coarse_slab(out_ref)], axis=0), operator(here, 1))
        to_out = same[0:256] + dot(of_in, operator(here, 1 + sign))
        to_in = same[256:512] + dot(of_out, operator(here, 1 - sign))
        put(spread.at[dy], to_out, to_in, same[512:])
        return carry

    lax.fori_loop(0, 7, at_dy, 0)
    for seg in range(5):
        rows = NY if seg < 4 else HY
        sums_ref[pl.ds(seg * NY, rows), :] = shifted(spread, seg)


def inner(where, out, into, tables):
    vmem = pl.BlockSpec(memory_space=pltpu.VMEM)
    return pl.pallas_call(
        inner_kernel,
        in_specs=[pl.BlockSpec(memory_space=pltpu.SMEM), vmem, vmem, pl.BlockSpec(memory_space=pl.ANY)],
        out_specs=vmem,
        out_shape=jax.ShapeDtypeStruct((FINE + HY, 256), F32),
        scratch_shapes=[
            pltpu.VMEM((7, 3, 7, 128, 128), BF16),
            pltpu.VMEM((7, SUMS + 16, 256), F32),
            pltpu.SemaphoreType.DMA((7,)),
        ],
        compiler_params=pltpu.CompilerParams(vmem_limit_bytes=VMEM),
        cost_estimate=pl.CostEstimate(flops=3_000_000_000, bytes_accessed=6_000_000, transcendentals=0),
        name="inner",
    )(where, out, into, tables)


def outer_kernel(where_ref, cross_ref, pair_ref, tables_ref, inner_ref, fine_ref, coarse_ref, tables, spread, sems):
    core = where_ref[1]

    def fetch(dy, side):
        return pltpu.make_async_copy(tables_ref.at[dy, 2 * side], tables.at[dy, side], sems.at[dy, side])

    for dy in range(7):
        for side in range(2):
            fetch(dy, side).start()
    clear_gaps(spread)
    partner = pair_ref.at[1 - core]

    def at_dy(dy, carry):
        for side in range(2):
            fetch(dy, side).wait()
        here = tables.at[dy]
        by_cross = dot(jnp.concatenate([slabs(cross_ref), coarse_slab(cross_ref)], axis=0), operator(here, core))
        by_pair = dot(jnp.concatenate([slabs(partner), coarse_slab(partner)], axis=0), operator(here, 1 - core))
        put(spread.at[dy], by_cross[0:256], by_pair[0:256], by_cross[256:] + by_pair[256:])
        return carry

    lax.fori_loop(0, 7, at_dy, 0)
    for q in range(2):
        pz = q + core - 2 * q * core
        for px in range(2):
            seg = 2 * q + px
            done = (inner_ref[pl.ds(seg * NY, NY), :] + shifted(spread, seg)).T
            for child in range(4):
                first = (2 * px + child // 2) * 4 + 2 * pz + child % 2
                fine_ref[pl.ds(first, COEF, stride=16), :] = done[child * SLOT : child * SLOT + COEF]
    done = (inner_ref[pl.ds(FINE, HY), :] + shifted(spread, 4)).T
    for child in range(4):
        coarse_ref[pl.ds(child, COEF, stride=4), :] = done[child * SLOT : child * SLOT + COEF]


def outer(where, cross, pair, tables, sums):
    vmem = pl.BlockSpec(memory_space=pltpu.VMEM)
    return pl.pallas_call(
        outer_kernel,
        in_specs=[pl.BlockSpec(memory_space=pltpu.SMEM), vmem, vmem, pl.BlockSpec(memory_space=pl.ANY), vmem],
        out_specs=[vmem, vmem],
        out_shape=[
            jax.ShapeDtypeStruct((16 * COEF, NY), F32),
            jax.ShapeDtypeStruct((4 * COEF, HY), F32),
        ],
        scratch_shapes=[
            pltpu.VMEM((7, 2, 7, 128, 128), BF16),
            pltpu.VMEM((7, SUMS + 16, 256), F32),
            pltpu.SemaphoreType.DMA((7, 2)),
        ],
        compiler_params=pltpu.CompilerParams(vmem_limit_bytes=VMEM),
        cost_estimate=pl.CostEstimate(flops=2_000_000_000, bytes_accessed=5_000_000, transcendentals=0),
        name="outer",
    )(where, cross, pair, tables, sums)


def exchange(array, axis, start):
    count = lax.axis_size(axis)
    there = [(i, i + 1) for i in range(start, count - 1, 2)]
    return lax.ppermute(array, axis, there + [(j, i) for i, j in there])


def shards(multipoles, translate_far, translate_up):
    where = jnp.stack([lax.axis_index("wide") % 2, lax.axis_index("narrow") % 2]).astype(jnp.int32)
    a = exchange(multipoles, "wide", 0)
    b = exchange(multipoles, "wide", 1)
    tables, pairs = make_tables(translate_far, translate_up.transpose(1, 0, 2).reshape(8 * COEF, COEF))
    flat = lambda brick: brick.reshape(16 * COEF, NY)
    out, into, parents = pack(where, flat(multipoles), flat(a), flat(b), pairs)
    cross = exchange(out, "narrow", 1)
    count = lax.axis_size("narrow")
    pair = lax.all_gather(into, "narrow", axis_index_groups=[[i, i + 1] for i in range(0, count, 2)])
    sums = inner(where, out, into, tables)
    fine, coarse = outer(where, cross, pair, tables, sums)
    return (
        fine.reshape(COEF, 4, 4, NY),
        parents.reshape(COEF, 2, 2, HY),
        coarse.reshape(COEF, 2, 2, HY),
    )


def solution(mesh):
    return jax.shard_map(
        shards,
        mesh=mesh,
        in_specs=(P(None, "wide", "narrow", None), P(), P()),
        out_specs=(
            P(None, "wide", "narrow", None),
            P(None, "wide", "narrow", None),
            P(None, "wide", "narrow", None),
        ),
        check_vma=False,
    )
```

```python
import jax
import jax.numpy as jnp
from jax import lax
from jax.experimental import pallas as pl
from jax.experimental.pallas import tpu as pltpu
from jax.sharding import PartitionSpec as P

F32 = jnp.float32
BF16 = jnp.bfloat16
NT = (((1,), (1,)), ((), ()))
COEF = 49
SLOT = 64
NY = 128
HY = 64
FINE = 4 * NY
ROWS = FINE + 3 * HY
SEG = NY + 8
SUMS = 4 * SEG + HY
VMEM = 20 * 2**20


def dot(a, b):
    return jnp.dot(a, b, preferred_element_type=F32)


def eye(n):
    rows = lax.broadcasted_iota(jnp.int32, (n, n), 0)
    cols = lax.broadcasted_iota(jnp.int32, (n, n), 1)
    return jnp.where(rows == cols, 1.0, 0.0).astype(BF16)


def core_parity():
    return lax.rem(lax.axis_index("narrow"), 2)


def turn(unit, bricks, brick, pair, zp):
    cells = []
    for cx in range(2):
        for cz in range(2):
            first = (2 * pair + cx) * 4 + 2 * zp + cz
            cells.append(bricks[brick, pl.ds(first, SLOT, stride=16), :].astype(BF16))
    cells = jnp.concatenate(cells, axis=0)
    return lax.dot_general(unit, cells, NT, preferred_element_type=F32).astype(BF16)


def to_parents(halves, at, low):
    z0, z1 = halves.at[at], halves.at[at + 1]
    first = z0[pl.ds(0, HY, stride=2), :] + pltpu.roll(z0[pl.ds(1, HY, stride=2), :], SLOT, 1)
    second = pltpu.roll(z1[pl.ds(0, HY, stride=2), :], SLOT, 1) + z1[pl.ds(1, HY, stride=2), :]
    return jnp.where(low, first, second).astype(BF16)


def lower_lanes():
    return lax.broadcasted_iota(jnp.int32, (HY, 128), 1) < SLOT


def early_kernel(
    far_hbm, own_hbm, up_hbm, tables_ref, slabs_ref, coarse_ref, pairs_ref, par_ref,
    far, own, up, bricks, wide, halves, shuffled, far_sems, sems,
):
    def fetch(dx):
        return pltpu.make_async_copy(far_hbm.at[dx], far.at[dx], far_sems.at[dx])

    get_own = pltpu.make_async_copy(own_hbm, own, sems.at[0])
    get_up = pltpu.make_async_copy(up_hbm, up, sems.at[1])
    get_own.start()
    get_up.start()
    for dx in range(7):
        fetch(dx).start()

    get_up.wait()
    wide[...] = up[...].astype(F32)
    pairs_ref[...] = jnp.zeros_like(pairs_ref)
    for child in range(8):
        block = wide[pl.ds(child, COEF, stride=8), :].astype(BF16)
        pairs_ref[pl.ds(SLOT * (child // 2), COEF), pl.ds(SLOT * (child % 2), COEF)] = block
    get_own.wait()
    bricks[0, pl.ds(16 * COEF, 16 * (SLOT - COEF)), :] = jnp.zeros((16 * (SLOT - COEF), NY), F32)
    bricks[0, pl.ds(0, 16 * COEF), :] = own[...].astype(F32)
    unit, low = eye(NY), lower_lanes()
    core = core_parity()
    for px in range(2):
        for q in range(2):
            zp = q + core - 2 * q * core
            turned = turn(unit, bricks, 0, px, zp)
            slabs_ref[pl.ds((2 * q + px) * NY, NY), :] = turned
            halves[2 * px + zp] = dot(turned, pairs_ref[...])
    for px in range(2):
        parent = to_parents(halves, 2 * px, low)
        coarse_ref[:, pl.ds(128 * px, 128)] = parent
        turned = lax.dot_general(unit, parent, NT, preferred_element_type=F32)
        for z in range(2):
            shuffled[pl.ds(2 * px + z, COEF, stride=4), :] = turned[z * SLOT : z * SLOT + COEF]
    par_ref[...] = shuffled[...].astype(BF16).reshape(COEF, 2, 2, HY)

    def at_dx(dx, carry):
        fetch(dx).wait()
        keep = jnp.where(jnp.abs(dx - 3) <= 1, 0.0, 1.0).astype(BF16)
        for dy in range(7):
            left, right = [], []
            for dz in range(7):
                block = far[dx, dz, dy]
                if abs(dz - 3) <= 1 and abs(dy - 3) <= 1:
                    block = block * keep
                block = jnp.pad(block, ((0, SLOT - COEF), (0, 128 - COEF)))
                left.append(block)
                right.append(jnp.concatenate([block[:, SLOT:], block[:, :SLOT]], axis=1))
            for sz in range(3):
                for cz in range(2):
                    tables_ref[dy, sz, dx, pl.ds(SLOT * cz, SLOT), :] = left[2 * sz + 1 + cz] + right[2 * sz + cz]
        return carry

    lax.fori_loop(0, 7, at_dx, 0)


def early(far, own, up):
    hbm = pl.BlockSpec(memory_space=pltpu.HBM)
    vmem = pl.BlockSpec(memory_space=pltpu.VMEM)
    return pl.pallas_call(
        early_kernel,
        in_specs=[hbm] * 3,
        out_specs=[vmem] * 5,
        out_shape=[
            pltpu.VMEM((7, 3, 7, 128, 128), BF16),
            pltpu.VMEM((FINE, 256), BF16),
            pltpu.VMEM((HY, 256), BF16),
            pltpu.VMEM((256, 128), BF16),
            jax.ShapeDtypeStruct((COEF, 2, 2, HY), BF16),
        ],
        scratch_shapes=[
            pltpu.VMEM((7, 7, 7, COEF, COEF), BF16),
            pltpu.VMEM((16 * COEF, NY), BF16),
            pltpu.VMEM((8 * COEF, COEF), BF16),
            pltpu.VMEM((1, 16 * SLOT, NY), F32),
            pltpu.VMEM((8 * COEF, COEF), F32),
            pltpu.VMEM((4, NY, 128), F32),
            pltpu.VMEM((4 * COEF, HY), F32),
            pltpu.SemaphoreType.DMA((7,)),
            pltpu.SemaphoreType.DMA((2,)),
        ],
        compiler_params=pltpu.CompilerParams(vmem_limit_bytes=VMEM),
        cost_estimate=pl.CostEstimate(flops=0, bytes_accessed=10_000_000, transcendentals=0),
        name="early",
    )(*[pltpu.with_memory_space_constraint(x, pltpu.HBM) for x in (far, own, up)])


def pack_kernel(a_ref, b_ref, slabs_ref, coarse_ref, pairs_ref, out_ref, in_ref, bricks, halves):
    odd, core = lax.rem(lax.axis_index("wide"), 2), core_parity()
    bricks[:, pl.ds(16 * COEF, 16 * (SLOT - COEF)), :] = jnp.zeros((2, 16 * (SLOT - COEF), NY), F32)
    bricks[1 - odd, pl.ds(0, 16 * COEF), :] = a_ref[...].astype(F32)
    bricks[odd, pl.ds(0, 16 * COEF), :] = b_ref[...].astype(F32)
    unit, low = eye(NY), lower_lanes()
    refs = (out_ref, in_ref)
    for q in range(2):
        refs[q][pl.ds(NY, 2 * NY), :] = slabs_ref[pl.ds(q * 2 * NY, 2 * NY), :]
        refs[q][pl.ds(FINE + HY, HY), :] = coarse_ref[...]
    for brick in range(2):
        for px in range(2):
            for q in range(2):
                zp = q + core - 2 * q * core
                turned = turn(unit, bricks, brick, px, zp)
                if px == 1 - brick:
                    refs[q][pl.ds(brick * 3 * NY, NY), :] = turned
                halves[4 * brick + 2 * px + zp] = dot(turned, pairs_ref[...])
    for brick in range(2):
        for px in range(2):
            parent = to_parents(halves, 4 * brick + 2 * px, low)
            for ref in refs:
                ref[pl.ds(FINE + 2 * brick * HY, HY), pl.ds(128 * px, 128)] = parent


def pack(a, b, own):
    vmem = pl.BlockSpec(memory_space=pltpu.VMEM)
    return pl.pallas_call(
        pack_kernel,
        in_specs=[vmem] * 5,
        out_specs=[vmem] * 2,
        out_shape=[jax.ShapeDtypeStruct((ROWS, 256), BF16)] * 2,
        scratch_shapes=[
            pltpu.VMEM((2, 16 * SLOT, NY), F32),
            pltpu.VMEM((8, NY, 128), F32),
        ],
        compiler_params=pltpu.CompilerParams(vmem_limit_bytes=VMEM),
        name="pack",
    )(a, b, *[pltpu.with_memory_space_constraint(x, pltpu.VMEM) for x in own])


def operator(tables, dy, at, skip=False):
    blocks = [tables[dy, at, dx] for dx in range(7)]
    return jnp.concatenate(
        [jnp.concatenate([blocks[e + 1], blocks[e]], axis=1) for e in range(6) if not (skip and e in (2, 3))],
        axis=0,
    )


def slabs(ref):
    part = [ref[pl.ds(x * NY, NY), :] for x in range(4)]
    return jnp.concatenate([jnp.concatenate(part[x : x + 3], axis=1) for x in range(2)], axis=0)


def coarse_slab(ref):
    return jnp.concatenate([ref[pl.ds(FINE + x * HY, HY), :] for x in range(3)], axis=1)


def clear_gaps(spread):
    for seg in range(5):
        spread[:, pl.ds(seg * SEG, 8), :] = jnp.zeros((7, 8, 256), F32)
    spread[:, pl.ds(8 + 4 * SEG + HY, 8), :] = jnp.zeros((7, 8, 256), F32)


def shifted(spread, seg):
    rows = NY if seg < 4 else HY
    even = lax.broadcasted_iota(jnp.int32, (rows, 256), 0) % 2 == 0
    total = None
    for dy in range(7):
        moved = spread[dy, pl.ds(5 + seg * SEG + dy, rows), :]
        if dy == 0:
            moved = jnp.where(even, 0.0, moved)
        if dy == 6:
            moved = jnp.where(even, moved, 0.0)
        total = moved if total is None else total + moved
    return total


def put(spread, fine_out, fine_in, coarse):
    for px in range(2):
        spread[pl.ds(8 + px * SEG, NY), :] = fine_out[px * NY : (px + 1) * NY]
        spread[pl.ds(8 + (2 + px) * SEG, NY), :] = fine_in[px * NY : (px + 1) * NY]
    spread[pl.ds(8 + 4 * SEG, HY), :] = coarse


def inner_kernel(out_ref, in_ref, tables, sums_ref, sources, spread):
    sign = 1 - 2 * core_parity()
    clear_gaps(spread)
    sources[...] = jnp.concatenate([slabs(out_ref), slabs(in_ref), coarse_slab(out_ref)], axis=0)
    for dy in range(7):
        if 2 <= dy <= 4:
            beside = jnp.concatenate([sources[:, 0:256], sources[:, 512:768]], axis=1)
            same = dot(beside, operator(tables, dy, 1, True))
        else:
            same = dot(sources[...], operator(tables, dy, 1))
        to_out = same[0:256] + dot(sources[256:512, :], operator(tables, dy, 1 + sign))
        to_in = same[256:512] + dot(sources[0:256, :], operator(tables, dy, 1 - sign))
        put(spread.at[dy], to_out, to_in, same[512:])
    for seg in range(5):
        rows = NY if seg < 4 else HY
        sums_ref[pl.ds(seg * NY, rows), :] = shifted(spread, seg)


def inner(out, into, tables):
    vmem = pl.BlockSpec(memory_space=pltpu.VMEM)
    return pl.pallas_call(
        inner_kernel,
        in_specs=[vmem, vmem, vmem],
        out_specs=vmem,
        out_shape=jax.ShapeDtypeStruct((FINE + HY, 256), F32),
        scratch_shapes=[
            pltpu.VMEM((FINE + HY, 768), BF16),
            pltpu.VMEM((7, SUMS + 16, 256), F32),
        ],
        compiler_params=pltpu.CompilerParams(vmem_limit_bytes=VMEM),
        cost_estimate=pl.CostEstimate(flops=3_000_000_000, bytes_accessed=6_000_000, transcendentals=0),
        name="inner",
    )(out, into, pltpu.with_memory_space_constraint(tables, pltpu.VMEM))


def outer_kernel(cross_ref, pair_ref, tables, inner_ref, fine_ref, coarse_ref, sources, spread, shuffled):
    core = core_parity()
    clear_gaps(spread)
    for at, ref in enumerate((cross_ref, pair_ref)):
        sources[at] = jnp.concatenate([slabs(ref), coarse_slab(ref)], axis=0)
    for dy in range(7):
        by_cross = dot(sources[0], operator(tables, dy, 2 * core))
        by_pair = dot(sources[1], operator(tables, dy, 2 - 2 * core))
        put(spread.at[dy], by_cross[0:256], by_pair[0:256], by_cross[256:] + by_pair[256:])
    for q in range(2):
        pz = q + core - 2 * q * core
        for px in range(2):
            seg = 2 * q + px
            done = (inner_ref[pl.ds(seg * NY, NY), :] + shifted(spread, seg)).T
            for child in range(4):
                first = (2 * px + child // 2) * 4 + 2 * pz + child % 2
                fine_ref[pl.ds(first, COEF, stride=16), :] = done[child * SLOT : child * SLOT + COEF]
    done = (inner_ref[pl.ds(FINE, HY), :] + shifted(spread, 4)).T
    for child in range(4):
        shuffled[pl.ds(child, COEF, stride=4), :] = done[child * SLOT : child * SLOT + COEF]
    coarse_ref[...] = shuffled[...].reshape(COEF, 2, 2, HY)


def outer(cross, pair, tables, sums):
    vmem = pl.BlockSpec(memory_space=pltpu.VMEM)
    return pl.pallas_call(
        outer_kernel,
        in_specs=[vmem, vmem, vmem, vmem],
        out_specs=[vmem, vmem],
        out_shape=[
            jax.ShapeDtypeStruct((16 * COEF, NY), F32),
            jax.ShapeDtypeStruct((COEF, 2, 2, HY), F32),
        ],
        scratch_shapes=[
            pltpu.VMEM((2, 256 + HY, 768), BF16),
            pltpu.VMEM((7, SUMS + 16, 256), F32),
            pltpu.VMEM((4 * COEF, HY), F32),
        ],
        compiler_params=pltpu.CompilerParams(vmem_limit_bytes=VMEM),
        cost_estimate=pl.CostEstimate(flops=2_000_000_000, bytes_accessed=5_000_000, transcendentals=0),
        name="outer",
    )(cross, pair, pltpu.with_memory_space_constraint(tables, pltpu.VMEM), sums)


def exchange(array, axis, start):
    count = lax.axis_size(axis)
    there = [(i, i + 1) for i in range(start, count - 1, 2)]
    return lax.ppermute(array, axis, there + [(j, i) for i, j in there])


def shards(multipoles, translate_far, translate_up):
    a = exchange(multipoles, "wide", 0)
    b = exchange(multipoles, "wide", 1)
    flat = lambda brick: brick.reshape(16 * COEF, NY)
    up = translate_up.transpose(1, 0, 2).reshape(8 * COEF, COEF)
    tables, *own, parents = early(translate_far, flat(multipoles), up)
    out, into = pack(flat(a), flat(b), own)
    cross = exchange(out, "narrow", 1)
    pair = exchange(into, "narrow", 0)
    sums = inner(out, into, tables)
    fine, coarse = outer(cross, pair, tables, sums)
    return fine.reshape(COEF, 4, 4, NY), parents, coarse


def solution(mesh):
    return jax.shard_map(
        shards,
        mesh=mesh,
        in_specs=(P(None, "wide", "narrow", None), P(), P()),
        out_specs=(
            P(None, "wide", "narrow", None),
            P(None, "wide", "narrow", None),
            P(None, "wide", "narrow", None),
        ),
        check_vma=False,
    )
```

```python
import jax
import jax.numpy as jnp
from jax import lax
from jax.experimental import pallas as pl
from jax.experimental.pallas import tpu as pltpu
from jax.sharding import PartitionSpec as P

F32 = jnp.float32
BF16 = jnp.bfloat16
NT = (((1,), (1,)), ((), ()))
COEF = 49
SLOT = 64
NY = 128
HY = 64
FINE = 4 * NY
ROWS = FINE + 3 * HY
SEG = NY + 8
VMEM = 20 * 2**20


def dot(a, b):
    return jnp.dot(a, b, preferred_element_type=F32)


def eye(n):
    rows = lax.broadcasted_iota(jnp.int32, (n, n), 0)
    cols = lax.broadcasted_iota(jnp.int32, (n, n), 1)
    return jnp.where(rows == cols, 1.0, 0.0).astype(BF16)


def core_parity():
    return lax.rem(lax.axis_index("narrow"), 2)


def turn(unit, bricks, brick, pair, zp):
    cells = []
    for cx in range(2):
        for cz in range(2):
            first = (2 * pair + cx) * 4 + 2 * zp + cz
            cells.append(bricks[brick, pl.ds(first, SLOT, stride=16), :].astype(BF16))
    cells = jnp.concatenate(cells, axis=0)
    return lax.dot_general(unit, cells, NT, preferred_element_type=F32).astype(BF16)


def to_parents(halves, at, low):
    z0, z1 = halves.at[at], halves.at[at + 1]
    first = z0[pl.ds(0, HY, stride=2), :] + pltpu.roll(z0[pl.ds(1, HY, stride=2), :], SLOT, 1)
    second = pltpu.roll(z1[pl.ds(0, HY, stride=2), :], SLOT, 1) + z1[pl.ds(1, HY, stride=2), :]
    return jnp.where(low, first, second).astype(BF16)


def lower_lanes():
    return lax.broadcasted_iota(jnp.int32, (HY, 128), 1) < SLOT


def early_kernel(
    far_hbm, own_hbm, up_hbm, tables_ref, slabs_ref, coarse_ref, pairs_ref, par_ref,
    far, own, up, bricks, wide, halves, shuffled, far_sems, sems,
):
    def fetch(dx):
        return pltpu.make_async_copy(far_hbm.at[dx], far.at[dx], far_sems.at[dx])

    get_own = pltpu.make_async_copy(own_hbm, own, sems.at[0])
    get_up = pltpu.make_async_copy(up_hbm, up, sems.at[1])
    get_own.start()
    get_up.start()
    for dx in range(7):
        fetch(dx).start()

    get_up.wait()
    wide[...] = up[...].astype(F32)
    pairs_ref[...] = jnp.zeros_like(pairs_ref)
    for child in range(8):
        block = wide[pl.ds(child, COEF, stride=8), :].astype(BF16)
        pairs_ref[pl.ds(SLOT * (child // 2), COEF), pl.ds(SLOT * (child % 2), COEF)] = block
    get_own.wait()
    bricks[0, pl.ds(16 * COEF, 16 * (SLOT - COEF)), :] = jnp.zeros((16 * (SLOT - COEF), NY), F32)
    bricks[0, pl.ds(0, 16 * COEF), :] = own[...].astype(F32)
    unit, low = eye(NY), lower_lanes()
    core = core_parity()
    for px in range(2):
        for q in range(2):
            zp = q + core - 2 * q * core
            turned = turn(unit, bricks, 0, px, zp)
            slabs_ref[pl.ds((2 * q + px) * NY, NY), :] = turned
            halves[2 * px + zp] = dot(turned, pairs_ref[...])
    for px in range(2):
        parent = to_parents(halves, 2 * px, low)
        coarse_ref[:, pl.ds(128 * px, 128)] = parent
        turned = lax.dot_general(unit, parent, NT, preferred_element_type=F32)
        for z in range(2):
            shuffled[pl.ds(2 * px + z, COEF, stride=4), :] = turned[z * SLOT : z * SLOT + COEF]
    par_ref[...] = shuffled[...].astype(BF16).reshape(COEF, 2, 2, HY)

    def at_dx(dx, carry):
        fetch(dx).wait()
        keep = jnp.where(jnp.abs(dx - 3) <= 1, 0.0, 1.0).astype(BF16)
        for dy in range(7):
            left, right = [], []
            for dz in range(7):
                block = far[dx, dz, dy]
                if abs(dz - 3) <= 1 and abs(dy - 3) <= 1:
                    block = block * keep
                block = jnp.pad(block, ((0, SLOT - COEF), (0, 128 - COEF)))
                left.append(block)
                right.append(jnp.concatenate([block[:, SLOT:], block[:, :SLOT]], axis=1))
            for sz in range(3):
                for cz in range(2):
                    tables_ref[dy, sz, dx, pl.ds(SLOT * cz, SLOT), :] = left[2 * sz + 1 + cz] + right[2 * sz + cz]
        return carry

    lax.fori_loop(0, 7, at_dx, 0)


def early(far, own, up):
    hbm = pl.BlockSpec(memory_space=pltpu.HBM)
    vmem = pl.BlockSpec(memory_space=pltpu.VMEM)
    return pl.pallas_call(
        early_kernel,
        in_specs=[hbm] * 3,
        out_specs=[vmem] * 5,
        out_shape=[
            pltpu.VMEM((7, 3, 7, 128, 128), BF16),
            pltpu.VMEM((FINE, 256), BF16),
            pltpu.VMEM((HY, 256), BF16),
            pltpu.VMEM((256, 128), BF16),
            jax.ShapeDtypeStruct((COEF, 2, 2, HY), BF16),
        ],
        scratch_shapes=[
            pltpu.VMEM((7, 7, 7, COEF, COEF), BF16),
            pltpu.VMEM((16 * COEF, NY), BF16),
            pltpu.VMEM((8 * COEF, COEF), BF16),
            pltpu.VMEM((1, 16 * SLOT, NY), F32),
            pltpu.VMEM((8 * COEF, COEF), F32),
            pltpu.VMEM((4, NY, 128), F32),
            pltpu.VMEM((4 * COEF, HY), F32),
            pltpu.SemaphoreType.DMA((7,)),
            pltpu.SemaphoreType.DMA((2,)),
        ],
        compiler_params=pltpu.CompilerParams(vmem_limit_bytes=VMEM),
        cost_estimate=pl.CostEstimate(flops=0, bytes_accessed=10_000_000, transcendentals=0),
        name="early",
    )(*[pltpu.with_memory_space_constraint(x, pltpu.HBM) for x in (far, own, up)])


def pack_kernel(b_ref, a_ref, slabs_ref, coarse_ref, pairs_ref, out_ref, in_ref, bricks, halves):
    odd, core = lax.rem(lax.axis_index("wide"), 2), core_parity()
    bricks[:, pl.ds(16 * COEF, 16 * (SLOT - COEF)), :] = jnp.zeros((2, 16 * (SLOT - COEF), NY), F32)
    bricks[1 - odd, pl.ds(0, 16 * COEF), :] = a_ref[...].astype(F32)
    bricks[odd, pl.ds(0, 16 * COEF), :] = b_ref[...].astype(F32)
    unit, low = eye(NY), lower_lanes()
    refs = (out_ref, in_ref)
    for q in range(2):
        refs[q][pl.ds(NY, 2 * NY), :] = slabs_ref[pl.ds(q * 2 * NY, 2 * NY), :]
        refs[q][pl.ds(FINE + HY, HY), :] = coarse_ref[...]
    for brick in range(2):
        for px in range(2):
            for q in range(2):
                zp = q + core - 2 * q * core
                turned = turn(unit, bricks, brick, px, zp)
                if px == 1 - brick:
                    refs[q][pl.ds(brick * 3 * NY, NY), :] = turned
                halves[4 * brick + 2 * px + zp] = dot(turned, pairs_ref[...])
    for brick in range(2):
        for px in range(2):
            parent = to_parents(halves, 4 * brick + 2 * px, low)
            for ref in refs:
                ref[pl.ds(FINE + 2 * brick * HY, HY), pl.ds(128 * px, 128)] = parent


def pack(a, b, own):
    vmem = pl.BlockSpec(memory_space=pltpu.VMEM)
    return pl.pallas_call(
        pack_kernel,
        in_specs=[vmem] * 5,
        out_specs=[vmem] * 2,
        out_shape=[jax.ShapeDtypeStruct((ROWS, 256), BF16)] * 2,
        scratch_shapes=[
            pltpu.VMEM((2, 16 * SLOT, NY), F32),
            pltpu.VMEM((8, NY, 128), F32),
        ],
        compiler_params=pltpu.CompilerParams(vmem_limit_bytes=VMEM),
        name="pack",
    )(a, b, *[pltpu.with_memory_space_constraint(x, pltpu.VMEM) for x in own])


def operator(tables, dy, at, skip=False):
    blocks = [tables[dy, at, dx] for dx in range(7)]
    return jnp.concatenate(
        [jnp.concatenate([blocks[e + 1], blocks[e]], axis=1) for e in range(6) if not (skip and e in (2, 3))],
        axis=0,
    )


def slabs(ref):
    part = [ref[pl.ds(x * NY, NY), :] for x in range(4)]
    return jnp.concatenate([jnp.concatenate(part[x : x + 3], axis=1) for x in range(2)], axis=0)


def coarse_slab(ref):
    return jnp.concatenate([ref[pl.ds(FINE + x * HY, HY), :] for x in range(3)], axis=1)


def clear_gaps(spread, count):
    for seg in range(count + 1):
        spread[:, pl.ds(seg * SEG, 8), :] = jnp.zeros((7, 8, 256), F32)
    spread[:, pl.ds(8 + count * SEG + HY, 8), :] = jnp.zeros((7, 8, 256), F32)


def shifted(spread, seg, rows):
    even = lax.broadcasted_iota(jnp.int32, (rows, 256), 0) % 2 == 0
    total = None
    for dy in range(7):
        moved = spread[dy, pl.ds(5 + seg * SEG + dy, rows), :]
        if dy == 0:
            moved = jnp.where(even, 0.0, moved)
        if dy == 6:
            moved = jnp.where(even, moved, 0.0)
        total = moved if total is None else total + moved
    return total


def put(spread, fine, coarse):
    for seg in range(fine.shape[0] // NY):
        spread[pl.ds(8 + seg * SEG, NY), :] = fine[seg * NY : (seg + 1) * NY]
    spread[pl.ds(8 + (fine.shape[0] // NY) * SEG, HY), :] = coarse


def finish(fine_ref, done, px, pz):
    for child in range(4):
        first = (2 * px + child // 2) * 4 + 2 * pz + child % 2
        fine_ref[pl.ds(first, COEF, stride=16), :] = done[child * SLOT : child * SLOT + COEF]


def inner_kernel(out_ref, in_ref, pair_ref, tables, part_ref, sums_ref, sources, beyond, spread):
    core = core_parity()
    sign = 1 - 2 * core
    clear_gaps(spread, 4)
    sources[...] = jnp.concatenate([slabs(out_ref), slabs(in_ref), coarse_slab(out_ref)], axis=0)
    beyond[...] = jnp.concatenate([slabs(pair_ref), coarse_slab(pair_ref)], axis=0)
    for dy in range(7):
        if 2 <= dy <= 4:
            beside = jnp.concatenate([sources[:, 0:256], sources[:, 512:768]], axis=1)
            same = dot(beside, operator(tables, dy, 1, True))
        else:
            same = dot(sources[...], operator(tables, dy, 1))
        ahead = dot(jnp.concatenate([sources[256:512, :], beyond[...]], axis=0), operator(tables, dy, 1 + sign))
        behind = dot(sources[0:256, :], operator(tables, dy, 1 - sign))
        to_out = same[0:256] + ahead[0:256]
        to_in = same[256:512] + ahead[256:512] + behind
        put(spread.at[dy], jnp.concatenate([to_out, to_in], axis=0), same[512:] + ahead[512:])
    for seg in range(2):
        sums_ref[pl.ds(seg * NY, NY), :] = shifted(spread, seg, NY)
        finish(part_ref, shifted(spread, 2 + seg, NY).T, seg, 1 - core)
    sums_ref[pl.ds(2 * NY, HY), :] = shifted(spread, 4, HY)


def inner(out, into, pair, tables):
    vmem = pl.BlockSpec(memory_space=pltpu.VMEM)
    return pl.pallas_call(
        inner_kernel,
        in_specs=[vmem] * 4,
        out_specs=[vmem] * 2,
        out_shape=[
            jax.ShapeDtypeStruct((16 * COEF, NY), F32),
            jax.ShapeDtypeStruct((2 * NY + HY, 256), F32),
        ],
        scratch_shapes=[
            pltpu.VMEM((FINE + HY, 768), BF16),
            pltpu.VMEM((2 * NY + HY, 768), BF16),
            pltpu.VMEM((7, 4 * SEG + HY + 16, 256), F32),
        ],
        compiler_params=pltpu.CompilerParams(vmem_limit_bytes=VMEM),
        cost_estimate=pl.CostEstimate(flops=3_000_000_000, bytes_accessed=6_000_000, transcendentals=0),
        name="inner",
    )(out, into, pair, pltpu.with_memory_space_constraint(tables, pltpu.VMEM))


def outer_kernel(cross_ref, tables, part_ref, sums_ref, fine_ref, coarse_ref, sources, spread, shuffled):
    core = core_parity()
    clear_gaps(spread, 2)
    sources[...] = jnp.concatenate([slabs(cross_ref), coarse_slab(cross_ref)], axis=0)
    for dy in range(7):
        found = dot(sources[...], operator(tables, dy, 2 * core))
        put(spread.at[dy], found[0:256], found[256:])
    fine_ref[...] = part_ref[...]
    for seg in range(2):
        finish(fine_ref, (sums_ref[pl.ds(seg * NY, NY), :] + shifted(spread, seg, NY)).T, seg, core)
    done = (sums_ref[pl.ds(2 * NY, HY), :] + shifted(spread, 2, HY)).T
    for child in range(4):
        shuffled[pl.ds(child, COEF, stride=4), :] = done[child * SLOT : child * SLOT + COEF]
    coarse_ref[...] = shuffled[...].reshape(COEF, 2, 2, HY)


def outer(cross, tables, part, sums):
    vmem = pl.BlockSpec(memory_space=pltpu.VMEM)
    return pl.pallas_call(
        outer_kernel,
        in_specs=[vmem] * 4,
        out_specs=[vmem, vmem],
        out_shape=[
            jax.ShapeDtypeStruct((16 * COEF, NY), F32),
            jax.ShapeDtypeStruct((COEF, 2, 2, HY), F32),
        ],
        scratch_shapes=[
            pltpu.VMEM((2 * NY + HY, 768), BF16),
            pltpu.VMEM((7, 2 * SEG + HY + 16, 256), F32),
            pltpu.VMEM((4 * COEF, HY), F32),
        ],
        compiler_params=pltpu.CompilerParams(vmem_limit_bytes=VMEM),
        cost_estimate=pl.CostEstimate(flops=1_000_000_000, bytes_accessed=5_000_000, transcendentals=0),
        name="outer",
    )(cross, pltpu.with_memory_space_constraint(tables, pltpu.VMEM), part, sums)


def exchange(array, axis, start):
    count = lax.axis_size(axis)
    there = [(i, i + 1) for i in range(start, count - 1, 2)]
    return lax.ppermute(array, axis, there + [(j, i) for i, j in there])


def shards(multipoles, translate_far, translate_up):
    b = exchange(multipoles, "wide", 1)
    a = exchange(multipoles, "wide", 0)
    flat = lambda brick: brick.reshape(16 * COEF, NY)
    up = translate_up.transpose(1, 0, 2).reshape(8 * COEF, COEF)
    tables, *own, parents = early(translate_far, flat(multipoles), up)
    out, into = pack(flat(b), flat(a), own)
    pair = exchange(into, "narrow", 0)
    cross = exchange(out, "narrow", 1)
    part, sums = inner(out, into, pair, tables)
    fine, coarse = outer(cross, tables, part, sums)
    return fine.reshape(COEF, 4, 4, NY), parents, coarse


def solution(mesh):
    return jax.shard_map(
        shards,
        mesh=mesh,
        in_specs=(P(None, "wide", "narrow", None), P(), P()),
        out_specs=(
            P(None, "wide", "narrow", None),
            P(None, "wide", "narrow", None),
            P(None, "wide", "narrow", None),
        ),
        check_vma=False,
    )
```

```python
import jax
import jax.numpy as jnp
from jax import lax
from jax.experimental import pallas as pl
from jax.experimental.pallas import tpu as pltpu
from jax.sharding import PartitionSpec as P

F32 = jnp.float32
BF16 = jnp.bfloat16
NT = (((1,), (1,)), ((), ()))
COEF = 49
SLOT = 64
NY = 128
HY = 64
FINE = 4 * NY
ROWS = FINE + 3 * HY
NEAR = 8 * COEF
SIDE = 496
SEG = NY + 8
VMEM = 20 * 2**20


def dot(a, b):
    return jnp.dot(a, b, preferred_element_type=F32)


def eye(n):
    rows = lax.broadcasted_iota(jnp.int32, (n, n), 0)
    cols = lax.broadcasted_iota(jnp.int32, (n, n), 1)
    return jnp.where(rows == cols, 1.0, 0.0).astype(BF16)


def core_parity():
    return lax.rem(lax.axis_index("narrow"), 2)


def turn(unit, cells):
    return lax.dot_general(unit, cells.astype(BF16), NT, preferred_element_type=F32)


def to_parents(halves, at, low):
    z0, z1 = halves.at[at], halves.at[at + 1]
    first = z0[pl.ds(0, HY, stride=2), :] + pltpu.roll(z0[pl.ds(1, HY, stride=2), :], SLOT, 1)
    second = pltpu.roll(z1[pl.ds(0, HY, stride=2), :], SLOT, 1) + z1[pl.ds(1, HY, stride=2), :]
    return jnp.where(low, first, second).astype(BF16)


def own_kernel(
    own_hbm, up_hbm, a_ref, b_ref, slabs_ref, coarse_ref,
    own, up, brick, packed, wide, pairs, halves, message, sems,
):
    odd = lax.rem(lax.axis_index("wide"), 2)
    get_up = pltpu.make_async_copy(up_hbm, up, sems.at[0])
    get_own = pltpu.make_async_copy(own_hbm, own, sems.at[1])
    get_own.start()
    get_up.start()
    pairs[...] = jnp.zeros_like(pairs)
    brick[pl.ds(16 * COEF, 16 * (SLOT - COEF)), :] = jnp.zeros((16 * (SLOT - COEF), NY), F32)
    unit = eye(NY)
    low = lax.broadcasted_iota(jnp.int32, (HY, 128), 1) < SLOT
    get_up.wait()
    wide[...] = up[...].astype(F32)
    for child in range(8):
        block = wide[pl.ds(child, COEF, stride=8), :].astype(BF16)
        pairs[pl.ds(SLOT * (child // 2), COEF), pl.ds(SLOT * (child % 2), COEF)] = block
    get_own.wait()
    brick[pl.ds(0, 16 * COEF), :] = own[...].astype(F32)
    cells = [brick[pl.ds(cell, SLOT, stride=16), :] for cell in range(16)]
    for cell in range(16):
        packed[pl.ds(COEF * cell, SLOT), :] = cells[cell]
    order = [(2 * px + cx) * 4 + 2 * zp + cz for px in range(2) for zp in range(2) for cx in range(2) for cz in range(2)]
    turned = turn(unit, jnp.concatenate([cells[cell] for cell in order], axis=0)).astype(BF16)
    parts = [turned[:, 256 * at : 256 * at + 256] for at in range(4)]
    sums = dot(jnp.concatenate(parts, axis=0), pairs[...])
    for at in range(4):
        slabs_ref[pl.ds(at * NY, NY), :] = parts[at]
        halves[at] = sums[at * NY : at * NY + NY]
    parents = [to_parents(halves, 2 * px, low) for px in range(2)]
    for px in range(2):
        coarse_ref[:, pl.ds(128 * px, 128)] = parents[px]
    turned = turn(unit, jnp.concatenate(parents, axis=0))
    message[pl.ds(NEAR, SLOT), :] = turned[0:SLOT]
    message[pl.ds(NEAR + COEF, SLOT), :] = turned[SLOT:128]
    for ref, half in ((b_ref, odd), (a_ref, 1 - odd)):
        message[pl.ds(0, NEAR), :] = packed[pl.ds(pl.multiple_of(half * NEAR, 8), NEAR), :]
        ref[...] = message[pl.ds(0, SIDE), :].astype(BF16)


def own_part(own, up):
    hbm = pl.BlockSpec(memory_space=pltpu.HBM)
    vmem = pl.BlockSpec(memory_space=pltpu.VMEM)
    return pl.pallas_call(
        own_kernel,
        in_specs=[hbm] * 2,
        out_specs=[vmem] * 4,
        out_shape=[
            pltpu.VMEM((SIDE, NY), BF16),
            pltpu.VMEM((SIDE, NY), BF16),
            pltpu.VMEM((FINE, 256), BF16),
            pltpu.VMEM((HY, 256), BF16),
        ],
        scratch_shapes=[
            pltpu.VMEM((16 * COEF, NY), BF16),
            pltpu.VMEM((8 * COEF, COEF), BF16),
            pltpu.VMEM((16 * SLOT, NY), F32),
            pltpu.VMEM((16 * COEF + 16, NY), F32),
            pltpu.VMEM((8 * COEF, COEF), F32),
            pltpu.VMEM((256, 128), BF16),
            pltpu.VMEM((4, NY, 128), F32),
            pltpu.VMEM((SIDE + 16, NY), F32),
            pltpu.SemaphoreType.DMA((2,)),
        ],
        compiler_params=pltpu.CompilerParams(vmem_limit_bytes=VMEM),
        name="own_part",
    )(*[pltpu.with_memory_space_constraint(x, pltpu.HBM) for x in (own, up)])


def tables_kernel(far_hbm, coarse_ref, tables_ref, par_ref, far, shuffled, sems):
    def fetch(dx):
        return pltpu.make_async_copy(far_hbm.at[dx], far.at[dx], sems.at[dx])

    for dx in range(7):
        fetch(dx).start()

    cells = jnp.concatenate([coarse_ref[:, pl.ds(128 * px, 128)] for px in range(2)], axis=0)
    turned = turn(eye(NY), cells)
    for px in range(2):
        for z in range(2):
            block = turned[z * SLOT : z * SLOT + COEF, px * HY : (px + 1) * HY]
            shuffled[pl.ds(2 * px + z, COEF, stride=4), :] = block
    par_ref[...] = shuffled[...].astype(BF16).reshape(COEF, 2, 2, HY)

    def at_dx(dx, carry):
        fetch(dx).wait()
        keep = jnp.where(jnp.abs(dx - 3) <= 1, 0.0, 1.0).astype(BF16)
        for dy in range(7):
            left, right = [], []
            for dz in range(7):
                block = far[dx, dz, dy]
                if abs(dz - 3) <= 1 and abs(dy - 3) <= 1:
                    block = block * keep
                block = jnp.pad(block, ((0, SLOT - COEF), (0, 128 - COEF)))
                left.append(block)
                right.append(jnp.concatenate([block[:, SLOT:], block[:, :SLOT]], axis=1))
            for sz in range(3):
                for cz in range(2):
                    tables_ref[dy, sz, dx, pl.ds(SLOT * cz, SLOT), :] = left[2 * sz + 1 + cz] + right[2 * sz + cz]
        return carry

    lax.fori_loop(0, 7, at_dx, 0)


def make_tables(far, coarse):
    vmem = pl.BlockSpec(memory_space=pltpu.VMEM)
    return pl.pallas_call(
        tables_kernel,
        in_specs=[pl.BlockSpec(memory_space=pltpu.HBM), vmem],
        out_specs=[vmem] * 2,
        out_shape=[
            pltpu.VMEM((7, 3, 7, 128, 128), BF16),
            jax.ShapeDtypeStruct((COEF, 2, 2, HY), BF16),
        ],
        scratch_shapes=[
            pltpu.VMEM((7, 7, 7, COEF, COEF), BF16),
            pltpu.VMEM((4 * COEF, HY), F32),
            pltpu.SemaphoreType.DMA((7,)),
        ],
        compiler_params=pltpu.CompilerParams(vmem_limit_bytes=VMEM),
        cost_estimate=pl.CostEstimate(flops=0, bytes_accessed=10_000_000, transcendentals=0),
        name="tables",
    )(pltpu.with_memory_space_constraint(far, pltpu.HBM), pltpu.with_memory_space_constraint(coarse, pltpu.VMEM))


def pack_kernel(b_ref, a_ref, slabs_ref, coarse_ref, tables_ref, out_ref, in_ref, bricks):
    odd, core = lax.rem(lax.axis_index("wide"), 2), core_parity()
    unit = eye(NY)
    refs = (out_ref, in_ref)
    for q in range(2):
        for px in range(2):
            row = pl.multiple_of((2 * px + q + core - 2 * q * core) * NY, NY)
            refs[q][pl.ds((1 + px) * NY, NY), :] = slabs_ref[pl.ds(row, NY), :]
        refs[q][pl.ds(FINE + HY, HY), :] = coarse_ref[...]
    for at, (side, above) in enumerate(((b_ref, odd), (a_ref, 1 - odd))):
        brick = bricks.at[at]
        brick[pl.ds(0, SIDE), :] = side[...].astype(F32)
        brick[pl.ds(SIDE, 16), :] = jnp.zeros((16, NY), F32)
        for q in range(2):
            zp = q + core - 2 * q * core
            cells = []
            for cx in range(2):
                for cz in range(2):
                    here = [brick[pl.ds(COEF * (4 * cx + 2 * z + cz), SLOT), :] for z in range(2)]
                    cells.append(jnp.where(zp == 0, here[0], here[1]))
            turned = turn(unit, jnp.concatenate(cells, axis=0)).astype(BF16)
            refs[q][pl.ds(pl.multiple_of(above * 3 * NY, NY), NY), :] = turned
        cells = jnp.concatenate([brick[pl.ds(NEAR + COEF * z, SLOT), :] for z in range(2)], axis=0)
        turned = turn(unit, cells).astype(BF16)
        for ref in refs:
            row = pl.multiple_of(FINE + above * 2 * HY, HY)
            for px in range(2):
                ref[pl.ds(row, HY), pl.ds(128 * px, 128)] = turned[px * HY : (px + 1) * HY]


def pack(b, a, slabs, coarse, tables):
    vmem = pl.BlockSpec(memory_space=pltpu.VMEM)
    return pl.pallas_call(
        pack_kernel,
        in_specs=[vmem] * 5,
        out_specs=[vmem] * 2,
        out_shape=[jax.ShapeDtypeStruct((ROWS, 256), BF16)] * 2,
        scratch_shapes=[pltpu.VMEM((2, SIDE + 16, NY), F32)],
        compiler_params=pltpu.CompilerParams(vmem_limit_bytes=VMEM),
        name="pack",
    )(b, a, *[pltpu.with_memory_space_constraint(x, pltpu.VMEM) for x in (slabs, coarse, tables)])


def operator(tables, dy, at, skip=False):
    blocks = [tables[dy, at, dx] for dx in range(7)]
    return jnp.concatenate(
        [jnp.concatenate([blocks[e + 1], blocks[e]], axis=1) for e in range(6) if not (skip and e in (2, 3))],
        axis=0,
    )


def slabs(ref):
    part = [ref[pl.ds(x * NY, NY), :] for x in range(4)]
    return jnp.concatenate([jnp.concatenate(part[x : x + 3], axis=1) for x in range(2)], axis=0)


def coarse_slab(ref):
    return jnp.concatenate([ref[pl.ds(FINE + x * HY, HY), :] for x in range(3)], axis=1)


def clear_gaps(spread, count):
    for seg in range(count + 1):
        spread[:, pl.ds(seg * SEG, 8), :] = jnp.zeros((7, 8, 256), F32)
    spread[:, pl.ds(8 + count * SEG + HY, 8), :] = jnp.zeros((7, 8, 256), F32)


def shifted(spread, seg, rows):
    even = lax.broadcasted_iota(jnp.int32, (rows, 256), 0) % 2 == 0
    total = None
    for dy in range(7):
        moved = spread[dy, pl.ds(5 + seg * SEG + dy, rows), :]
        if dy == 0:
            moved = jnp.where(even, 0.0, moved)
        if dy == 6:
            moved = jnp.where(even, moved, 0.0)
        total = moved if total is None else total + moved
    return total


def put(spread, fine, coarse):
    for seg in range(fine.shape[0] // NY):
        spread[pl.ds(8 + seg * SEG, NY), :] = fine[seg * NY : (seg + 1) * NY]
    spread[pl.ds(8 + (fine.shape[0] // NY) * SEG, HY), :] = coarse


def finish(fine_ref, done, px, pz):
    for child in range(4):
        first = (2 * px + child // 2) * 4 + 2 * pz + child % 2
        fine_ref[pl.ds(first, COEF, stride=16), :] = done[child * SLOT : child * SLOT + COEF]


def inner_kernel(out_ref, in_ref, pair_ref, tables, part_ref, sums_ref, sources, beyond, spread):
    core = core_parity()
    sign = 1 - 2 * core
    clear_gaps(spread, 4)
    sources[...] = jnp.concatenate([slabs(out_ref), slabs(in_ref), coarse_slab(out_ref)], axis=0)
    beyond[...] = jnp.concatenate([slabs(pair_ref), coarse_slab(pair_ref)], axis=0)
    for dy in range(7):
        if 2 <= dy <= 4:
            beside = jnp.concatenate([sources[:, 0:256], sources[:, 512:768]], axis=1)
            same = dot(beside, operator(tables, dy, 1, True))
        else:
            same = dot(sources[...], operator(tables, dy, 1))
        ahead = dot(jnp.concatenate([sources[256:512, :], beyond[...]], axis=0), operator(tables, dy, 1 + sign))
        behind = dot(sources[0:256, :], operator(tables, dy, 1 - sign))
        to_out = same[0:256] + ahead[0:256]
        to_in = same[256:512] + ahead[256:512] + behind
        put(spread.at[dy], jnp.concatenate([to_out, to_in], axis=0), same[512:] + ahead[512:])
    for seg in range(2):
        sums_ref[pl.ds(seg * NY, NY), :] = shifted(spread, seg, NY)
        finish(part_ref, shifted(spread, 2 + seg, NY).T, seg, 1 - core)
    sums_ref[pl.ds(2 * NY, HY), :] = shifted(spread, 4, HY)


def inner(out, into, pair, tables):
    vmem = pl.BlockSpec(memory_space=pltpu.VMEM)
    return pl.pallas_call(
        inner_kernel,
        in_specs=[vmem] * 4,
        out_specs=[vmem] * 2,
        out_shape=[
            jax.ShapeDtypeStruct((16 * COEF, NY), F32),
            jax.ShapeDtypeStruct((2 * NY + HY, 256), F32),
        ],
        scratch_shapes=[
            pltpu.VMEM((FINE + HY, 768), BF16),
            pltpu.VMEM((2 * NY + HY, 768), BF16),
            pltpu.VMEM((7, 4 * SEG + HY + 16, 256), F32),
        ],
        compiler_params=pltpu.CompilerParams(vmem_limit_bytes=VMEM),
        cost_estimate=pl.CostEstimate(flops=3_000_000_000, bytes_accessed=6_000_000, transcendentals=0),
        name="inner",
    )(out, into, pair, pltpu.with_memory_space_constraint(tables, pltpu.VMEM))


def outer_kernel(cross_ref, tables, part_ref, sums_ref, fine_ref, coarse_ref, sources, spread, shuffled):
    core = core_parity()
    clear_gaps(spread, 2)
    sources[...] = jnp.concatenate([slabs(cross_ref), coarse_slab(cross_ref)], axis=0)
    for dy in range(7):
        found = dot(sources[...], operator(tables, dy, 2 * core))
        put(spread.at[dy], found[0:256], found[256:])
    fine_ref[...] = part_ref[...]
    for seg in range(2):
        finish(fine_ref, (sums_ref[pl.ds(seg * NY, NY), :] + shifted(spread, seg, NY)).T, seg, core)
    done = (sums_ref[pl.ds(2 * NY, HY), :] + shifted(spread, 2, HY)).T
    for child in range(4):
        shuffled[pl.ds(child, COEF, stride=4), :] = done[child * SLOT : child * SLOT + COEF]
    coarse_ref[...] = shuffled[...].reshape(COEF, 2, 2, HY)


def outer(cross, tables, part, sums):
    vmem = pl.BlockSpec(memory_space=pltpu.VMEM)
    return pl.pallas_call(
        outer_kernel,
        in_specs=[vmem] * 4,
        out_specs=[vmem, vmem],
        out_shape=[
            jax.ShapeDtypeStruct((16 * COEF, NY), F32),
            jax.ShapeDtypeStruct((COEF, 2, 2, HY), F32),
        ],
        scratch_shapes=[
            pltpu.VMEM((2 * NY + HY, 768), BF16),
            pltpu.VMEM((7, 2 * SEG + HY + 16, 256), F32),
            pltpu.VMEM((4 * COEF, HY), F32),
        ],
        compiler_params=pltpu.CompilerParams(vmem_limit_bytes=VMEM),
        cost_estimate=pl.CostEstimate(flops=1_000_000_000, bytes_accessed=5_000_000, transcendentals=0),
        name="outer",
    )(cross, pltpu.with_memory_space_constraint(tables, pltpu.VMEM), part, sums)


def exchange(array, axis, start):
    count = lax.axis_size(axis)
    there = [(i, i + 1) for i in range(start, count - 1, 2)]
    return lax.ppermute(array, axis, there + [(j, i) for i, j in there])


def shards(multipoles, translate_far, translate_up):
    up = translate_up.transpose(1, 0, 2).reshape(8 * COEF, COEF)
    to_a, to_b, slabs, coarse = own_part(multipoles.reshape(16 * COEF, NY), up)
    b = exchange(to_b, "wide", 1)
    a = exchange(to_a, "wide", 0)
    tables, parents = make_tables(translate_far, coarse)
    out, into = pack(b, a, slabs, coarse, tables)
    pair = exchange(into, "narrow", 0)
    cross = exchange(out, "narrow", 1)
    part, sums = inner(out, into, pair, tables)
    fine, coarse_locals = outer(cross, tables, part, sums)
    return fine.reshape(COEF, 4, 4, NY), parents, coarse_locals


def solution(mesh):
    return jax.shard_map(
        shards,
        mesh=mesh,
        in_specs=(P(None, "wide", "narrow", None), P(), P()),
        out_specs=(
            P(None, "wide", "narrow", None),
            P(None, "wide", "narrow", None),
            P(None, "wide", "narrow", None),
        ),
        check_vma=False,
    )
```

```python
import jax
import jax.numpy as jnp
from jax import lax
from jax.experimental import pallas as pl
from jax.experimental.pallas import tpu as pltpu
from jax.sharding import PartitionSpec as P

F32 = jnp.float32
BF16 = jnp.bfloat16
NT = (((1,), (1,)), ((), ()))
COEF = 49
SLOT = 64
NY = 128
HY = 64
BLOCK = 208
PAIR = 112
SIDE = 2 * BLOCK + PAIR
COLUMN = 4 * BLOCK
ROWS = COLUMN + 3 * PAIR
SEG = NY + 8
VMEM = 20 * 2**20


def dot(a, b):
    return jnp.dot(a, b, preferred_element_type=F32)


def eye(n):
    rows = lax.broadcasted_iota(jnp.int32, (n, n), 0)
    cols = lax.broadcasted_iota(jnp.int32, (n, n), 1)
    return jnp.where(rows == cols, 1.0, 0.0).astype(BF16)


def core_parity():
    return lax.rem(lax.axis_index("narrow"), 2)


def turn(unit, cells):
    return lax.dot_general(unit, cells.astype(BF16), NT, preferred_element_type=F32)


def to_parents(halves, at, low):
    z0, z1 = halves.at[at], halves.at[at + 1]
    first = z0[pl.ds(0, HY, stride=2), :] + pltpu.roll(z0[pl.ds(1, HY, stride=2), :], SLOT, 1)
    second = pltpu.roll(z1[pl.ds(0, HY, stride=2), :], SLOT, 1) + z1[pl.ds(1, HY, stride=2), :]
    return jnp.where(low, first, second).astype(BF16)


def own_kernel(
    own_hbm, up_hbm, a_ref, b_ref, packed_ref, coarse_ref,
    own, up, brick, packed, wide, pairs, halves, parents_t, sems,
):
    odd = lax.rem(lax.axis_index("wide"), 2)
    get_up = pltpu.make_async_copy(up_hbm, up, sems.at[0])
    get_own = pltpu.make_async_copy(own_hbm, own, sems.at[1])
    get_own.start()
    get_up.start()
    pairs[...] = jnp.zeros_like(pairs)
    brick[pl.ds(16 * COEF, 16 * (SLOT - COEF)), :] = jnp.zeros((16 * (SLOT - COEF), NY), F32)
    unit = eye(NY)
    low = lax.broadcasted_iota(jnp.int32, (HY, 128), 1) < SLOT
    get_up.wait()
    wide[...] = up[...].astype(F32)
    for child in range(8):
        block = wide[pl.ds(child, COEF, stride=8), :].astype(BF16)
        pairs[pl.ds(SLOT * (child // 2), COEF), pl.ds(SLOT * (child % 2), COEF)] = block
    get_own.wait()
    brick[pl.ds(0, 16 * COEF), :] = own[...].astype(F32)
    cells = [brick[pl.ds(cell, SLOT, stride=16), :] for cell in range(16)]
    order = [(2 * px + cx) * 4 + 2 * zp + cz for px in range(2) for zp in range(2) for cx in range(2) for cz in range(2)]
    for at, cell in enumerate(order):
        packed[pl.ds(BLOCK * (at // 4) + COEF * (at % 4), SLOT), :] = cells[cell]
    turned = turn(unit, jnp.concatenate([cells[cell] for cell in order], axis=0)).astype(BF16)
    packed_ref[...] = packed[pl.ds(0, COLUMN), :].astype(BF16)
    a_ref[pl.ds(0, 2 * BLOCK), :] = packed_ref[pl.ds(pl.multiple_of((1 - odd) * 2 * BLOCK, 16), 2 * BLOCK), :]
    b_ref[pl.ds(0, 2 * BLOCK), :] = packed_ref[pl.ds(pl.multiple_of(odd * 2 * BLOCK, 16), 2 * BLOCK), :]
    sums = dot(jnp.concatenate([turned[:, 256 * at : 256 * at + 256] for at in range(4)], axis=0), pairs[...])
    for at in range(4):
        halves[at] = sums[at * NY : at * NY + NY]
    parents = [to_parents(halves, 2 * px, low) for px in range(2)]
    coarse = jnp.concatenate(parents, axis=0)
    coarse_ref[...] = coarse
    turned = turn(unit, coarse)
    parents_t[pl.ds(0, SLOT), :] = turned[0:SLOT]
    parents_t[pl.ds(COEF, SLOT), :] = turned[SLOT:128]
    for ref in (a_ref, b_ref):
        ref[pl.ds(2 * BLOCK, PAIR), :] = parents_t[pl.ds(0, PAIR), :].astype(BF16)


def own_part(own, up):
    hbm = pl.BlockSpec(memory_space=pltpu.HBM)
    vmem = pl.BlockSpec(memory_space=pltpu.VMEM)
    return pl.pallas_call(
        own_kernel,
        in_specs=[hbm] * 2,
        out_specs=[vmem] * 4,
        out_shape=[
            pltpu.VMEM((SIDE, NY), BF16),
            pltpu.VMEM((SIDE, NY), BF16),
            pltpu.VMEM((COLUMN, NY), BF16),
            pltpu.VMEM((128, 128), BF16),
        ],
        scratch_shapes=[
            pltpu.VMEM((16 * COEF, NY), BF16),
            pltpu.VMEM((8 * COEF, COEF), BF16),
            pltpu.VMEM((16 * SLOT, NY), F32),
            pltpu.VMEM((COLUMN + 16, NY), F32),
            pltpu.VMEM((8 * COEF, COEF), F32),
            pltpu.VMEM((256, 128), BF16),
            pltpu.VMEM((4, NY, 128), F32),
            pltpu.VMEM((120, NY), F32),
            pltpu.SemaphoreType.DMA((2,)),
        ],
        compiler_params=pltpu.CompilerParams(vmem_limit_bytes=VMEM),
        name="own_part",
    )(*[pltpu.with_memory_space_constraint(x, pltpu.HBM) for x in (own, up)])


def tables_kernel(far_hbm, coarse_ref, tables_ref, par_ref, far, shuffled, sems):
    def fetch(dx):
        return pltpu.make_async_copy(far_hbm.at[dx], far.at[dx], sems.at[dx])

    for dx in range(7):
        fetch(dx).start()

    turned = turn(eye(NY), coarse_ref[...])
    for px in range(2):
        for z in range(2):
            block = turned[z * SLOT : z * SLOT + COEF, px * HY : (px + 1) * HY]
            shuffled[pl.ds(2 * px + z, COEF, stride=4), :] = block
    par_ref[...] = shuffled[...].astype(BF16).reshape(COEF, 2, 2, HY)

    def at_dx(dx, carry):
        fetch(dx).wait()
        keep = jnp.where(jnp.abs(dx - 3) <= 1, 0.0, 1.0).astype(BF16)
        for dy in range(7):
            left, right = [], []
            for dz in range(7):
                block = far[dx, dz, dy]
                if abs(dz - 3) <= 1 and abs(dy - 3) <= 1:
                    block = block * keep
                block = jnp.pad(block, ((0, SLOT - COEF), (0, 128 - COEF)))
                left.append(block)
                right.append(jnp.concatenate([block[:, SLOT:], block[:, :SLOT]], axis=1))
            for sz in range(3):
                for cz in range(2):
                    tables_ref[dy, sz, dx, pl.ds(SLOT * cz, SLOT), :] = left[2 * sz + 1 + cz] + right[2 * sz + cz]
        return carry

    lax.fori_loop(0, 7, at_dx, 0)


def make_tables(far, coarse):
    vmem = pl.BlockSpec(memory_space=pltpu.VMEM)
    return pl.pallas_call(
        tables_kernel,
        in_specs=[pl.BlockSpec(memory_space=pltpu.HBM), vmem],
        out_specs=[vmem] * 2,
        out_shape=[
            pltpu.VMEM((7, 3, 7, 128, 128), BF16),
            jax.ShapeDtypeStruct((COEF, 2, 2, HY), BF16),
        ],
        scratch_shapes=[
            pltpu.VMEM((7, 7, 7, COEF, COEF), BF16),
            pltpu.VMEM((4 * COEF, HY), F32),
            pltpu.SemaphoreType.DMA((7,)),
        ],
        compiler_params=pltpu.CompilerParams(vmem_limit_bytes=VMEM),
        cost_estimate=pl.CostEstimate(flops=0, bytes_accessed=10_000_000, transcendentals=0),
        name="tables",
    )(pltpu.with_memory_space_constraint(far, pltpu.HBM), pltpu.with_memory_space_constraint(coarse, pltpu.VMEM))


def pack_kernel(b_ref, a_ref, packed_ref, mine_ref, tables_ref, out_ref, in_ref):
    odd, core = lax.rem(lax.axis_index("wide"), 2), core_parity()
    for q, ref in enumerate((out_ref, in_ref)):
        zp = q + core - 2 * q * core
        for px in range(2):
            row = pl.multiple_of((2 * px + zp) * BLOCK, 16)
            ref[pl.ds((1 + px) * BLOCK, BLOCK), :] = packed_ref[pl.ds(row, BLOCK), :]
        ref[pl.ds(COLUMN + PAIR, PAIR), :] = mine_ref[pl.ds(2 * BLOCK, PAIR), :]
        for side, above in ((b_ref, odd), (a_ref, 1 - odd)):
            row = pl.multiple_of(above * 3 * BLOCK, 16)
            ref[pl.ds(row, BLOCK), :] = side[pl.ds(pl.multiple_of(zp * BLOCK, 16), BLOCK), :]
            row = pl.multiple_of(COLUMN + above * 2 * PAIR, 16)
            ref[pl.ds(row, PAIR), :] = side[pl.ds(2 * BLOCK, PAIR), :]


def pack(b, a, packed, mine, tables):
    vmem = pl.BlockSpec(memory_space=pltpu.VMEM)
    return pl.pallas_call(
        pack_kernel,
        in_specs=[vmem] * 5,
        out_specs=[vmem] * 2,
        out_shape=[jax.ShapeDtypeStruct((ROWS, NY), BF16)] * 2,
        compiler_params=pltpu.CompilerParams(vmem_limit_bytes=VMEM),
        name="pack",
    )(b, a, *[pltpu.with_memory_space_constraint(x, pltpu.VMEM) for x in (packed, mine, tables)])


def operator(tables, dy, at, skip=False):
    blocks = [tables[dy, at, dx] for dx in range(7)]
    return jnp.concatenate(
        [jnp.concatenate([blocks[e + 1], blocks[e]], axis=1) for e in range(6) if not (skip and e in (2, 3))],
        axis=0,
    )


def sources_of(ref, rows):
    rows[pl.ds(0, ROWS), :] = ref[...].astype(F32)
    rows[pl.ds(ROWS, 16), :] = jnp.zeros((16, NY), F32)
    cells = [rows[pl.ds(BLOCK * at + COEF * cell, SLOT), :] for at in range(4) for cell in range(4)]
    cells += [rows[pl.ds(COLUMN + PAIR * at + COEF * z, SLOT), :] for at in range(3) for z in range(2)]
    turned = turn(eye(NY), jnp.concatenate(cells, axis=0)).astype(BF16)
    fine = jnp.concatenate([turned[:, 0:768], turned[:, 256:1024]], axis=0)
    parts = [turned[px * HY : (px + 1) * HY, 1024 + 128 * at : 1152 + 128 * at] for at in range(3) for px in range(2)]
    return fine, jnp.concatenate(parts, axis=1)


def clear_gaps(spread, count):
    for seg in range(count + 1):
        spread[:, pl.ds(seg * SEG, 8), :] = jnp.zeros((7, 8, 256), F32)
    spread[:, pl.ds(8 + count * SEG + HY, 8), :] = jnp.zeros((7, 8, 256), F32)


def shifted(spread, seg, rows):
    even = lax.broadcasted_iota(jnp.int32, (rows, 256), 0) % 2 == 0
    total = None
    for dy in range(7):
        moved = spread[dy, pl.ds(5 + seg * SEG + dy, rows), :]
        if dy == 0:
            moved = jnp.where(even, 0.0, moved)
        if dy == 6:
            moved = jnp.where(even, moved, 0.0)
        total = moved if total is None else total + moved
    return total


def put(spread, fine, coarse):
    for seg in range(fine.shape[0] // NY):
        spread[pl.ds(8 + seg * SEG, NY), :] = fine[seg * NY : (seg + 1) * NY]
    spread[pl.ds(8 + (fine.shape[0] // NY) * SEG, HY), :] = coarse


def finish(fine_ref, done, px, pz):
    for child in range(4):
        first = (2 * px + child // 2) * 4 + 2 * pz + child % 2
        fine_ref[pl.ds(first, COEF, stride=16), :] = done[child * SLOT : child * SLOT + COEF]


def inner_kernel(out_ref, in_ref, pair_ref, tables, part_ref, sums_ref, sources, beyond, spread, rows):
    core = core_parity()
    sign = 1 - 2 * core
    clear_gaps(spread, 4)
    for at, ref in enumerate((out_ref, in_ref, pair_ref)):
        fine, coarse = sources_of(ref, rows.at[at])
        if at < 2:
            sources[pl.ds(256 * at, 256), :] = fine
            sources[pl.ds(512, HY), :] = coarse
        else:
            beyond[pl.ds(0, 256), :] = fine
            beyond[pl.ds(256, HY), :] = coarse
    for dy in range(7):
        if 2 <= dy <= 4:
            beside = jnp.concatenate([sources[:, 0:256], sources[:, 512:768]], axis=1)
            same = dot(beside, operator(tables, dy, 1, True))
        else:
            same = dot(sources[...], operator(tables, dy, 1))
        ahead = dot(jnp.concatenate([sources[256:512, :], beyond[...]], axis=0), operator(tables, dy, 1 + sign))
        behind = dot(sources[0:256, :], operator(tables, dy, 1 - sign))
        to_out = same[0:256] + ahead[0:256]
        to_in = same[256:512] + ahead[256:512] + behind
        put(spread.at[dy], jnp.concatenate([to_out, to_in], axis=0), same[512:] + ahead[512:])
    for seg in range(2):
        sums_ref[pl.ds(seg * NY, NY), :] = shifted(spread, seg, NY)
        finish(part_ref, shifted(spread, 2 + seg, NY).T, seg, 1 - core)
    sums_ref[pl.ds(2 * NY, HY), :] = shifted(spread, 4, HY)


def inner(out, into, pair, tables):
    vmem = pl.BlockSpec(memory_space=pltpu.VMEM)
    return pl.pallas_call(
        inner_kernel,
        in_specs=[vmem] * 4,
        out_specs=[vmem] * 2,
        out_shape=[
            jax.ShapeDtypeStruct((16 * COEF, NY), F32),
            jax.ShapeDtypeStruct((2 * NY + HY, 256), F32),
        ],
        scratch_shapes=[
            pltpu.VMEM((4 * NY + HY, 768), BF16),
            pltpu.VMEM((2 * NY + HY, 768), BF16),
            pltpu.VMEM((7, 4 * SEG + HY + 16, 256), F32),
            pltpu.VMEM((3, ROWS + 16, NY), F32),
        ],
        compiler_params=pltpu.CompilerParams(vmem_limit_bytes=VMEM),
        cost_estimate=pl.CostEstimate(flops=3_000_000_000, bytes_accessed=6_000_000, transcendentals=0),
        name="inner",
    )(out, into, pair, pltpu.with_memory_space_constraint(tables, pltpu.VMEM))


def outer_kernel(cross_ref, tables, part_ref, sums_ref, fine_ref, coarse_ref, sources, spread, shuffled, rows):
    core = core_parity()
    clear_gaps(spread, 2)
    sources[...] = jnp.concatenate(sources_of(cross_ref, rows), axis=0)
    for dy in range(7):
        found = dot(sources[...], operator(tables, dy, 2 * core))
        put(spread.at[dy], found[0:256], found[256:])
    fine_ref[...] = part_ref[...]
    for seg in range(2):
        finish(fine_ref, (sums_ref[pl.ds(seg * NY, NY), :] + shifted(spread, seg, NY)).T, seg, core)
    done = (sums_ref[pl.ds(2 * NY, HY), :] + shifted(spread, 2, HY)).T
    for child in range(4):
        shuffled[pl.ds(child, COEF, stride=4), :] = done[child * SLOT : child * SLOT + COEF]
    coarse_ref[...] = shuffled[...].reshape(COEF, 2, 2, HY)


def outer(cross, tables, part, sums):
    vmem = pl.BlockSpec(memory_space=pltpu.VMEM)
    return pl.pallas_call(
        outer_kernel,
        in_specs=[vmem] * 4,
        out_specs=[vmem, vmem],
        out_shape=[
            jax.ShapeDtypeStruct((16 * COEF, NY), F32),
            jax.ShapeDtypeStruct((COEF, 2, 2, HY), F32),
        ],
        scratch_shapes=[
            pltpu.VMEM((2 * NY + HY, 768), BF16),
            pltpu.VMEM((7, 2 * SEG + HY + 16, 256), F32),
            pltpu.VMEM((4 * COEF, HY), F32),
            pltpu.VMEM((ROWS + 16, NY), F32),
        ],
        compiler_params=pltpu.CompilerParams(vmem_limit_bytes=VMEM),
        cost_estimate=pl.CostEstimate(flops=1_000_000_000, bytes_accessed=5_000_000, transcendentals=0),
        name="outer",
    )(cross, pltpu.with_memory_space_constraint(tables, pltpu.VMEM), part, sums)


def exchange(array, axis, start):
    count = lax.axis_size(axis)
    there = [(i, i + 1) for i in range(start, count - 1, 2)]
    return lax.ppermute(array, axis, there + [(j, i) for i, j in there])


def shards(multipoles, translate_far, translate_up):
    up = translate_up.transpose(1, 0, 2).reshape(8 * COEF, COEF)
    to_a, to_b, packed, coarse = own_part(multipoles.reshape(16 * COEF, NY), up)
    b = exchange(to_b, "wide", 1)
    a = exchange(to_a, "wide", 0)
    tables, parents = make_tables(translate_far, coarse)
    out, into = pack(b, a, packed, to_b, tables)
    pair = exchange(into, "narrow", 0)
    cross = exchange(out, "narrow", 1)
    part, sums = inner(out, into, pair, tables)
    fine, coarse_locals = outer(cross, tables, part, sums)
    return fine.reshape(COEF, 4, 4, NY), parents, coarse_locals


def solution(mesh):
    return jax.shard_map(
        shards,
        mesh=mesh,
        in_specs=(P(None, "wide", "narrow", None), P(), P()),
        out_specs=(
            P(None, "wide", "narrow", None),
            P(None, "wide", "narrow", None),
            P(None, "wide", "narrow", None),
        ),
        check_vma=False,
    )
```

```python
import jax
import jax.numpy as jnp
from jax import lax
from jax.experimental import pallas as pl
from jax.experimental.pallas import tpu as pltpu
from jax.sharding import PartitionSpec as P

F32 = jnp.float32
BF16 = jnp.bfloat16
NT = (((1,), (1,)), ((), ()))
COEF = 49
SLOT = 64
NY = 128
HY = 64
BLOCK = 208
PAIR = 112
SIDE = 2 * BLOCK + PAIR
COLUMN = 4 * BLOCK
ROWS = COLUMN + 3 * PAIR
SEG = NY + 8
VMEM = 20 * 2**20


def dot(a, b):
    return jnp.dot(a, b, preferred_element_type=F32)


def eye(n):
    rows = lax.broadcasted_iota(jnp.int32, (n, n), 0)
    cols = lax.broadcasted_iota(jnp.int32, (n, n), 1)
    return jnp.where(rows == cols, 1.0, 0.0).astype(BF16)


def core_parity():
    return lax.rem(lax.axis_index("narrow"), 2)


def turn(unit, cells):
    return lax.dot_general(unit, cells.astype(BF16), NT, preferred_element_type=F32)


def own_kernel(
    own_hbm, up_hbm, a_ref, b_ref, packed_ref, coarse_ref,
    own, up, brick, packed, wide, pairs, parents_t, sems,
):
    odd = lax.rem(lax.axis_index("wide"), 2)
    get_up = pltpu.make_async_copy(up_hbm, up, sems.at[0])
    get_own = pltpu.make_async_copy(own_hbm, own, sems.at[1])
    get_own.start()
    get_up.start()
    pairs[...] = jnp.zeros_like(pairs)
    brick[pl.ds(16 * COEF, 16 * (SLOT - COEF)), :] = jnp.zeros((16 * (SLOT - COEF), NY), F32)
    get_up.wait()
    wide[...] = up[...].astype(F32)
    for child in range(8):
        block = wide[pl.ds(child, COEF, stride=8), :].astype(BF16)
        pairs[pl.ds(SLOT * (child // 2), COEF), pl.ds(SLOT * (child % 2), COEF)] = block
    pairs_t = pairs[...].T
    get_own.wait()
    brick[pl.ds(0, 16 * COEF), :] = own[...].astype(F32)
    cells = [brick[pl.ds(cell, SLOT, stride=16), :] for cell in range(16)]
    order = [(2 * px + cx) * 4 + 2 * zp + cz for px in range(2) for zp in range(2) for cx in range(2) for cz in range(2)]
    for at, cell in enumerate(order):
        packed[pl.ds(BLOCK * (at // 4) + COEF * (at % 4), SLOT), :] = cells[cell]
    packed_ref[...] = packed[pl.ds(0, COLUMN), :].astype(BF16)
    a_ref[pl.ds(0, 2 * BLOCK), :] = packed_ref[pl.ds(pl.multiple_of((1 - odd) * 2 * BLOCK, 16), 2 * BLOCK), :]
    b_ref[pl.ds(0, 2 * BLOCK), :] = packed_ref[pl.ds(pl.multiple_of(odd * 2 * BLOCK, 16), 2 * BLOCK), :]
    lane = lax.broadcasted_iota(jnp.int32, (SLOT, NY), 1)
    even = 2 * lax.rem(lane, HY)
    for zp in range(2):
        found = []
        for px in range(2):
            part = jnp.concatenate([cells[cell] for cell in order[8 * px + 4 * zp : 8 * px + 4 * zp + 4]], axis=0)
            both = dot(pairs_t, part.astype(BF16))
            first = jnp.take_along_axis(both[0:SLOT], even, axis=1, mode="promise_in_bounds")
            second = jnp.take_along_axis(both[SLOT:128], even + 1, axis=1, mode="promise_in_bounds")
            found.append(first + second)
        parents = jnp.where(lane < HY, found[0], found[1])
        parents_t[pl.ds(COEF * zp, SLOT), :] = parents
        coarse_ref[pl.ds(SLOT * zp, SLOT), :] = parents.astype(BF16)
    for ref in (a_ref, b_ref):
        ref[pl.ds(2 * BLOCK, PAIR), :] = parents_t[pl.ds(0, PAIR), :].astype(BF16)


def own_part(own, up):
    hbm = pl.BlockSpec(memory_space=pltpu.HBM)
    vmem = pl.BlockSpec(memory_space=pltpu.VMEM)
    return pl.pallas_call(
        own_kernel,
        in_specs=[hbm] * 2,
        out_specs=[vmem] * 4,
        out_shape=[
            pltpu.VMEM((SIDE, NY), BF16),
            pltpu.VMEM((SIDE, NY), BF16),
            pltpu.VMEM((COLUMN, NY), BF16),
            pltpu.VMEM((128, 128), BF16),
        ],
        scratch_shapes=[
            pltpu.VMEM((16 * COEF, NY), BF16),
            pltpu.VMEM((8 * COEF, COEF), BF16),
            pltpu.VMEM((16 * SLOT, NY), F32),
            pltpu.VMEM((COLUMN + 16, NY), F32),
            pltpu.VMEM((8 * COEF, COEF), F32),
            pltpu.VMEM((256, 128), BF16),
            pltpu.VMEM((120, NY), F32),
            pltpu.SemaphoreType.DMA((2,)),
        ],
        compiler_params=pltpu.CompilerParams(vmem_limit_bytes=VMEM),
        name="own_part",
    )(*[pltpu.with_memory_space_constraint(x, pltpu.HBM) for x in (own, up)])


def tables_kernel(far_hbm, coarse_ref, tables_ref, par_ref, far, shuffled, sems):
    def fetch(dx):
        return pltpu.make_async_copy(far_hbm.at[dx], far.at[dx], sems.at[dx])

    for dx in range(7):
        fetch(dx).start()

    turned = coarse_ref[...].astype(F32)
    for px in range(2):
        for z in range(2):
            block = turned[z * SLOT : z * SLOT + COEF, px * HY : (px + 1) * HY]
            shuffled[pl.ds(2 * px + z, COEF, stride=4), :] = block
    par_ref[...] = shuffled[...].astype(BF16).reshape(COEF, 2, 2, HY)

    def at_dx(dx, carry):
        fetch(dx).wait()
        keep = jnp.where(jnp.abs(dx - 3) <= 1, 0.0, 1.0).astype(BF16)
        for dy in range(7):
            left, right = [], []
            for dz in range(7):
                block = far[dx, dz, dy]
                if abs(dz - 3) <= 1 and abs(dy - 3) <= 1:
                    block = block * keep
                block = jnp.pad(block, ((0, SLOT - COEF), (0, 128 - COEF)))
                left.append(block)
                right.append(jnp.concatenate([block[:, SLOT:], block[:, :SLOT]], axis=1))
            for sz in range(3):
                for cz in range(2):
                    tables_ref[dy, sz, dx, pl.ds(SLOT * cz, SLOT), :] = left[2 * sz + 1 + cz] + right[2 * sz + cz]
        return carry

    lax.fori_loop(0, 7, at_dx, 0)


def make_tables(far, coarse):
    vmem = pl.BlockSpec(memory_space=pltpu.VMEM)
    return pl.pallas_call(
        tables_kernel,
        in_specs=[pl.BlockSpec(memory_space=pltpu.HBM), vmem],
        out_specs=[vmem] * 2,
        out_shape=[
            pltpu.VMEM((7, 3, 7, 128, 128), BF16),
            jax.ShapeDtypeStruct((COEF, 2, 2, HY), BF16),
        ],
        scratch_shapes=[
            pltpu.VMEM((7, 7, 7, COEF, COEF), BF16),
            pltpu.VMEM((4 * COEF, HY), F32),
            pltpu.SemaphoreType.DMA((7,)),
        ],
        compiler_params=pltpu.CompilerParams(vmem_limit_bytes=VMEM),
        cost_estimate=pl.CostEstimate(flops=0, bytes_accessed=10_000_000, transcendentals=0),
        name="tables",
    )(pltpu.with_memory_space_constraint(far, pltpu.HBM), pltpu.with_memory_space_constraint(coarse, pltpu.VMEM))


def pack_kernel(b_ref, a_ref, packed_ref, mine_ref, tables_ref, out_ref, in_ref):
    odd, core = lax.rem(lax.axis_index("wide"), 2), core_parity()
    for q, ref in enumerate((out_ref, in_ref)):
        zp = q + core - 2 * q * core
        for px in range(2):
            row = pl.multiple_of((2 * px + zp) * BLOCK, 16)
            ref[pl.ds((1 + px) * BLOCK, BLOCK), :] = packed_ref[pl.ds(row, BLOCK), :]
        ref[pl.ds(COLUMN + PAIR, PAIR), :] = mine_ref[pl.ds(2 * BLOCK, PAIR), :]
        for side, above in ((b_ref, odd), (a_ref, 1 - odd)):
            row = pl.multiple_of(above * 3 * BLOCK, 16)
            ref[pl.ds(row, BLOCK), :] = side[pl.ds(pl.multiple_of(zp * BLOCK, 16), BLOCK), :]
            row = pl.multiple_of(COLUMN + above * 2 * PAIR, 16)
            ref[pl.ds(row, PAIR), :] = side[pl.ds(2 * BLOCK, PAIR), :]


def pack(b, a, packed, mine, tables):
    vmem = pl.BlockSpec(memory_space=pltpu.VMEM)
    return pl.pallas_call(
        pack_kernel,
        in_specs=[vmem] * 5,
        out_specs=[vmem] * 2,
        out_shape=[jax.ShapeDtypeStruct((ROWS, NY), BF16)] * 2,
        compiler_params=pltpu.CompilerParams(vmem_limit_bytes=VMEM),
        name="pack",
    )(b, a, *[pltpu.with_memory_space_constraint(x, pltpu.VMEM) for x in (packed, mine, tables)])


def operator(tables, dy, at, skip=False):
    blocks = [tables[dy, at, dx] for dx in range(7)]
    return jnp.concatenate(
        [jnp.concatenate([blocks[e + 1], blocks[e]], axis=1) for e in range(6) if not (skip and e in (2, 3))],
        axis=0,
    )


def sources_of(ref, rows):
    rows[pl.ds(0, ROWS), :] = ref[...].astype(F32)
    rows[pl.ds(ROWS, 16), :] = jnp.zeros((16, NY), F32)
    cells = [rows[pl.ds(BLOCK * at + COEF * cell, SLOT), :] for at in range(4) for cell in range(4)]
    cells += [rows[pl.ds(COLUMN + PAIR * at + COEF * z, SLOT), :] for at in range(3) for z in range(2)]
    turned = turn(eye(NY), jnp.concatenate(cells, axis=0)).astype(BF16)
    fine = jnp.concatenate([turned[:, 0:768], turned[:, 256:1024]], axis=0)
    parts = [turned[px * HY : (px + 1) * HY, 1024 + 128 * at : 1152 + 128 * at] for at in range(3) for px in range(2)]
    return fine, jnp.concatenate(parts, axis=1)


def clear_gaps(spread, count):
    for seg in range(count + 1):
        spread[:, pl.ds(seg * SEG, 8), :] = jnp.zeros((7, 8, 256), F32)
    spread[:, pl.ds(8 + count * SEG + HY, 8), :] = jnp.zeros((7, 8, 256), F32)


def shifted(spread, seg, rows):
    even = lax.broadcasted_iota(jnp.int32, (rows, 256), 0) % 2 == 0
    total = None
    for dy in range(7):
        moved = spread[dy, pl.ds(5 + seg * SEG + dy, rows), :]
        if dy == 0:
            moved = jnp.where(even, 0.0, moved)
        if dy == 6:
            moved = jnp.where(even, moved, 0.0)
        total = moved if total is None else total + moved
    return total


def put(spread, fine, coarse):
    for seg in range(fine.shape[0] // NY):
        spread[pl.ds(8 + seg * SEG, NY), :] = fine[seg * NY : (seg + 1) * NY]
    spread[pl.ds(8 + (fine.shape[0] // NY) * SEG, HY), :] = coarse


def finish(fine_ref, done, px, pz):
    for child in range(4):
        first = (2 * px + child // 2) * 4 + 2 * pz + child % 2
        fine_ref[pl.ds(first, COEF, stride=16), :] = done[child * SLOT : child * SLOT + COEF]


def inner_kernel(out_ref, in_ref, pair_ref, tables, part_ref, sums_ref, sources, beyond, spread, rows):
    core = core_parity()
    sign = 1 - 2 * core
    clear_gaps(spread, 4)
    for at, ref in enumerate((out_ref, in_ref, pair_ref)):
        fine, coarse = sources_of(ref, rows.at[at])
        if at < 2:
            sources[pl.ds(256 * at, 256), :] = fine
            sources[pl.ds(512, HY), :] = coarse
        else:
            beyond[pl.ds(0, 256), :] = fine
            beyond[pl.ds(256, HY), :] = coarse
    for dy in range(7):
        if 2 <= dy <= 4:
            beside = jnp.concatenate([sources[:, 0:256], sources[:, 512:768]], axis=1)
            same = dot(beside, operator(tables, dy, 1, True))
        else:
            same = dot(sources[...], operator(tables, dy, 1))
        ahead = dot(jnp.concatenate([sources[256:512, :], beyond[...]], axis=0), operator(tables, dy, 1 + sign))
        behind = dot(sources[0:256, :], operator(tables, dy, 1 - sign))
        to_out = same[0:256] + ahead[0:256]
        to_in = same[256:512] + ahead[256:512] + behind
        put(spread.at[dy], jnp.concatenate([to_out, to_in], axis=0), same[512:] + ahead[512:])
    for seg in range(2):
        sums_ref[pl.ds(seg * NY, NY), :] = shifted(spread, seg, NY)
        finish(part_ref, shifted(spread, 2 + seg, NY).T, seg, 1 - core)
    sums_ref[pl.ds(2 * NY, HY), :] = shifted(spread, 4, HY)


def inner(out, into, pair, tables):
    vmem = pl.BlockSpec(memory_space=pltpu.VMEM)
    return pl.pallas_call(
        inner_kernel,
        in_specs=[vmem] * 4,
        out_specs=[vmem] * 2,
        out_shape=[
            jax.ShapeDtypeStruct((16 * COEF, NY), F32),
            jax.ShapeDtypeStruct((2 * NY + HY, 256), F32),
        ],
        scratch_shapes=[
            pltpu.VMEM((4 * NY + HY, 768), BF16),
            pltpu.VMEM((2 * NY + HY, 768), BF16),
            pltpu.VMEM((7, 4 * SEG + HY + 16, 256), F32),
            pltpu.VMEM((3, ROWS + 16, NY), F32),
        ],
        compiler_params=pltpu.CompilerParams(vmem_limit_bytes=VMEM),
        cost_estimate=pl.CostEstimate(flops=3_000_000_000, bytes_accessed=6_000_000, transcendentals=0),
        name="inner",
    )(out, into, pair, pltpu.with_memory_space_constraint(tables, pltpu.VMEM))


def outer_kernel(cross_ref, tables, part_ref, sums_ref, fine_ref, coarse_ref, sources, spread, shuffled, rows):
    core = core_parity()
    clear_gaps(spread, 2)
    sources[...] = jnp.concatenate(sources_of(cross_ref, rows), axis=0)
    for dy in range(7):
        found = dot(sources[...], operator(tables, dy, 2 * core))
        put(spread.at[dy], found[0:256], found[256:])
    fine_ref[...] = part_ref[...]
    for seg in range(2):
        finish(fine_ref, (sums_ref[pl.ds(seg * NY, NY), :] + shifted(spread, seg, NY)).T, seg, core)
    done = (sums_ref[pl.ds(2 * NY, HY), :] + shifted(spread, 2, HY)).T
    for child in range(4):
        shuffled[pl.ds(child, COEF, stride=4), :] = done[child * SLOT : child * SLOT + COEF]
    coarse_ref[...] = shuffled[...].reshape(COEF, 2, 2, HY)


def outer(cross, tables, part, sums):
    vmem = pl.BlockSpec(memory_space=pltpu.VMEM)
    return pl.pallas_call(
        outer_kernel,
        in_specs=[vmem] * 4,
        out_specs=[vmem, vmem],
        out_shape=[
            jax.ShapeDtypeStruct((16 * COEF, NY), F32),
            jax.ShapeDtypeStruct((COEF, 2, 2, HY), F32),
        ],
        scratch_shapes=[
            pltpu.VMEM((2 * NY + HY, 768), BF16),
            pltpu.VMEM((7, 2 * SEG + HY + 16, 256), F32),
            pltpu.VMEM((4 * COEF, HY), F32),
            pltpu.VMEM((ROWS + 16, NY), F32),
        ],
        compiler_params=pltpu.CompilerParams(vmem_limit_bytes=VMEM),
        cost_estimate=pl.CostEstimate(flops=1_000_000_000, bytes_accessed=5_000_000, transcendentals=0),
        name="outer",
    )(cross, pltpu.with_memory_space_constraint(tables, pltpu.VMEM), part, sums)


def exchange(array, axis, start):
    count = lax.axis_size(axis)
    there = [(i, i + 1) for i in range(start, count - 1, 2)]
    return lax.ppermute(array, axis, there + [(j, i) for i, j in there])


def shards(multipoles, translate_far, translate_up):
    up = translate_up.transpose(1, 0, 2).reshape(8 * COEF, COEF)
    to_a, to_b, packed, coarse = own_part(multipoles.reshape(16 * COEF, NY), up)
    b = exchange(to_b, "wide", 1)
    a = exchange(to_a, "wide", 0)
    tables, parents = make_tables(translate_far, coarse)
    out, into = pack(b, a, packed, to_b, tables)
    pair = exchange(into, "narrow", 0)
    cross = exchange(out, "narrow", 1)
    part, sums = inner(out, into, pair, tables)
    fine, coarse_locals = outer(cross, tables, part, sums)
    return fine.reshape(COEF, 4, 4, NY), parents, coarse_locals


def solution(mesh):
    return jax.shard_map(
        shards,
        mesh=mesh,
        in_specs=(P(None, "wide", "narrow", None), P(), P()),
        out_specs=(
            P(None, "wide", "narrow", None),
            P(None, "wide", "narrow", None),
            P(None, "wide", "narrow", None),
        ),
        check_vma=False,
    )
```

```python
import jax
import jax.numpy as jnp
from jax import lax
from jax.experimental import pallas as pl
from jax.experimental.pallas import tpu as pltpu
from jax.sharding import PartitionSpec as P

F32 = jnp.float32
BF16 = jnp.bfloat16
NT = (((1,), (1,)), ((), ()))
COEF = 49
SLOT = 64
NY = 128
HY = 64
BLOCK = 208
PAIR = 112
SIDE = 2 * BLOCK + PAIR
COLUMN = 4 * BLOCK
ROWS = COLUMN + 3 * PAIR
SEG = NY + 8
VMEM = 20 * 2**20


def dot(a, b):
    return jnp.dot(a, b, preferred_element_type=F32)


def eye(n):
    rows = lax.broadcasted_iota(jnp.int32, (n, n), 0)
    cols = lax.broadcasted_iota(jnp.int32, (n, n), 1)
    return jnp.where(rows == cols, 1.0, 0.0).astype(BF16)


def core_parity():
    return lax.rem(lax.axis_index("narrow"), 2)


def turn(unit, cells):
    return lax.dot_general(unit, cells.astype(BF16), NT, preferred_element_type=F32)


def own_kernel(
    own_hbm, up_hbm, a_ref, b_ref, packed_ref, coarse_ref,
    own, up, brick, packed, wide, pairs, parents_t, sems,
):
    odd = lax.rem(lax.axis_index("wide"), 2)
    get_up = pltpu.make_async_copy(up_hbm, up, sems.at[0])
    get_own = pltpu.make_async_copy(own_hbm, own, sems.at[1])
    get_own.start()
    get_up.start()
    pairs[...] = jnp.zeros_like(pairs)
    brick[pl.ds(16 * COEF, 16 * (SLOT - COEF)), :] = jnp.zeros((16 * (SLOT - COEF), NY), F32)
    get_own.wait()
    get_up.wait()
    wide[...] = up[...].astype(F32)
    for child in range(8):
        block = wide[pl.ds(child, COEF, stride=8), :].astype(BF16)
        pairs[pl.ds(SLOT * (child // 2), COEF), pl.ds(SLOT * (child % 2), COEF)] = block
    pairs_t = pairs[...].T
    brick[pl.ds(0, 16 * COEF), :] = own[...].astype(F32)
    cells = [brick[pl.ds(cell, SLOT, stride=16), :] for cell in range(16)]
    order = [(2 * px + cx) * 4 + 2 * zp + cz for px in range(2) for zp in range(2) for cx in range(2) for cz in range(2)]
    for at, cell in enumerate(order):
        packed[pl.ds(BLOCK * (at // 4) + COEF * (at % 4), SLOT), :] = cells[cell]
    packed_ref[...] = packed[pl.ds(0, COLUMN), :].astype(BF16)
    a_ref[pl.ds(0, 2 * BLOCK), :] = packed_ref[pl.ds(pl.multiple_of((1 - odd) * 2 * BLOCK, 16), 2 * BLOCK), :]
    b_ref[pl.ds(0, 2 * BLOCK), :] = packed_ref[pl.ds(pl.multiple_of(odd * 2 * BLOCK, 16), 2 * BLOCK), :]
    lane = lax.broadcasted_iota(jnp.int32, (SLOT, NY), 1)
    even = 2 * lax.rem(lane, HY)
    for zp in range(2):
        found = []
        for px in range(2):
            part = jnp.concatenate([cells[cell] for cell in order[8 * px + 4 * zp : 8 * px + 4 * zp + 4]], axis=0)
            both = dot(pairs_t, part.astype(BF16))
            first = jnp.take_along_axis(both[0:SLOT], even, axis=1, mode="promise_in_bounds")
            second = jnp.take_along_axis(both[SLOT:128], even + 1, axis=1, mode="promise_in_bounds")
            found.append(first + second)
        parents = jnp.where(lane < HY, found[0], found[1])
        parents_t[pl.ds(COEF * zp, SLOT), :] = parents
        coarse_ref[pl.ds(SLOT * zp, SLOT), :] = parents.astype(BF16)
    for ref in (a_ref, b_ref):
        ref[pl.ds(2 * BLOCK, PAIR), :] = parents_t[pl.ds(0, PAIR), :].astype(BF16)


def own_part(own, up):
    hbm = pl.BlockSpec(memory_space=pltpu.HBM)
    vmem = pl.BlockSpec(memory_space=pltpu.VMEM)
    return pl.pallas_call(
        own_kernel,
        in_specs=[hbm] * 2,
        out_specs=[vmem] * 4,
        out_shape=[
            pltpu.VMEM((SIDE, NY), BF16),
            pltpu.VMEM((SIDE, NY), BF16),
            pltpu.VMEM((COLUMN, NY), BF16),
            pltpu.VMEM((128, 128), BF16),
        ],
        scratch_shapes=[
            pltpu.VMEM((16 * COEF, NY), BF16),
            pltpu.VMEM((8 * COEF, COEF), BF16),
            pltpu.VMEM((16 * SLOT, NY), F32),
            pltpu.VMEM((COLUMN + 16, NY), F32),
            pltpu.VMEM((8 * COEF, COEF), F32),
            pltpu.VMEM((256, 128), BF16),
            pltpu.VMEM((120, NY), F32),
            pltpu.SemaphoreType.DMA((2,)),
        ],
        compiler_params=pltpu.CompilerParams(vmem_limit_bytes=VMEM),
        name="own_part",
    )(*[pltpu.with_memory_space_constraint(x, pltpu.HBM) for x in (own, up)])


def tables_kernel(far_hbm, coarse_ref, tables_ref, par_ref, far, shuffled, sems):
    def fetch(dx):
        return pltpu.make_async_copy(far_hbm.at[dx], far.at[dx], sems.at[dx])

    for dx in range(7):
        fetch(dx).start()

    turned = coarse_ref[...].astype(F32)
    for px in range(2):
        for z in range(2):
            block = turned[z * SLOT : z * SLOT + COEF, px * HY : (px + 1) * HY]
            shuffled[pl.ds(2 * px + z, COEF, stride=4), :] = block
    par_ref[...] = shuffled[...].astype(BF16).reshape(COEF, 2, 2, HY)

    def at_dx(dx, carry):
        fetch(dx).wait()
        keep = jnp.where(jnp.abs(dx - 3) <= 1, 0.0, 1.0).astype(BF16)
        for dy in range(7):
            left, right = [], []
            for dz in range(7):
                block = far[dx, dz, dy]
                if abs(dz - 3) <= 1 and abs(dy - 3) <= 1:
                    block = block * keep
                block = jnp.pad(block, ((0, SLOT - COEF), (0, 128 - COEF)))
                left.append(block)
                right.append(jnp.concatenate([block[:, SLOT:], block[:, :SLOT]], axis=1))
            for sz in range(3):
                for cz in range(2):
                    tables_ref[dy, sz, dx, pl.ds(SLOT * cz, SLOT), :] = left[2 * sz + 1 + cz] + right[2 * sz + cz]
        return carry

    lax.fori_loop(0, 7, at_dx, 0)


def make_tables(far, coarse):
    vmem = pl.BlockSpec(memory_space=pltpu.VMEM)
    return pl.pallas_call(
        tables_kernel,
        in_specs=[pl.BlockSpec(memory_space=pltpu.HBM), vmem],
        out_specs=[vmem] * 2,
        out_shape=[
            pltpu.VMEM((7, 3, 7, 128, 128), BF16),
            jax.ShapeDtypeStruct((COEF, 2, 2, HY), BF16),
        ],
        scratch_shapes=[
            pltpu.VMEM((7, 7, 7, COEF, COEF), BF16),
            pltpu.VMEM((4 * COEF, HY), F32),
            pltpu.SemaphoreType.DMA((7,)),
        ],
        compiler_params=pltpu.CompilerParams(vmem_limit_bytes=VMEM),
        cost_estimate=pl.CostEstimate(flops=0, bytes_accessed=10_000_000, transcendentals=0),
        name="tables",
    )(pltpu.with_memory_space_constraint(far, pltpu.HBM), pltpu.with_memory_space_constraint(coarse, pltpu.VMEM))


def pack_kernel(b_ref, a_ref, packed_ref, mine_ref, tables_ref, out_ref, in_ref):
    odd, core = lax.rem(lax.axis_index("wide"), 2), core_parity()
    for q, ref in enumerate((out_ref, in_ref)):
        zp = q + core - 2 * q * core
        for px in range(2):
            row = pl.multiple_of((2 * px + zp) * BLOCK, 16)
            ref[pl.ds((1 + px) * BLOCK, BLOCK), :] = packed_ref[pl.ds(row, BLOCK), :]
        ref[pl.ds(COLUMN + PAIR, PAIR), :] = mine_ref[pl.ds(2 * BLOCK, PAIR), :]
        for side, above in ((b_ref, odd), (a_ref, 1 - odd)):
            row = pl.multiple_of(above * 3 * BLOCK, 16)
            ref[pl.ds(row, BLOCK), :] = side[pl.ds(pl.multiple_of(zp * BLOCK, 16), BLOCK), :]
            row = pl.multiple_of(COLUMN + above * 2 * PAIR, 16)
            ref[pl.ds(row, PAIR), :] = side[pl.ds(2 * BLOCK, PAIR), :]


def pack(b, a, packed, mine, tables):
    vmem = pl.BlockSpec(memory_space=pltpu.VMEM)
    return pl.pallas_call(
        pack_kernel,
        in_specs=[vmem] * 5,
        out_specs=[vmem] * 2,
        out_shape=[jax.ShapeDtypeStruct((ROWS, NY), BF16)] * 2,
        compiler_params=pltpu.CompilerParams(vmem_limit_bytes=VMEM),
        name="pack",
    )(b, a, *[pltpu.with_memory_space_constraint(x, pltpu.VMEM) for x in (packed, mine, tables)])


def operator(tables, dy, at, skip=False):
    blocks = [tables[dy, at, dx] for dx in range(7)]
    return jnp.concatenate(
        [jnp.concatenate([blocks[e + 1], blocks[e]], axis=1) for e in range(6) if not (skip and e in (2, 3))],
        axis=0,
    )


def sources_of(ref, rows):
    rows[pl.ds(0, ROWS), :] = ref[...].astype(F32)
    rows[pl.ds(ROWS, 16), :] = jnp.zeros((16, NY), F32)
    cells = [rows[pl.ds(BLOCK * at + COEF * cell, SLOT), :] for at in range(4) for cell in range(4)]
    cells += [rows[pl.ds(COLUMN + PAIR * at + COEF * z, SLOT), :] for at in range(3) for z in range(2)]
    turned = turn(eye(NY), jnp.concatenate(cells, axis=0)).astype(BF16)
    fine = jnp.concatenate([turned[:, 0:768], turned[:, 256:1024]], axis=0)
    parts = [turned[px * HY : (px + 1) * HY, 1024 + 128 * at : 1152 + 128 * at] for at in range(3) for px in range(2)]
    return fine, jnp.concatenate(parts, axis=1)


def clear_gaps(spread, count):
    for seg in range(count + 1):
        spread[:, pl.ds(seg * SEG, 8), :] = jnp.zeros((7, 8, 256), F32)
    spread[:, pl.ds(8 + count * SEG + HY, 8), :] = jnp.zeros((7, 8, 256), F32)


def shifted(spread, seg, rows):
    even = lax.broadcasted_iota(jnp.int32, (rows, 256), 0) % 2 == 0
    total = None
    for dy in range(7):
        moved = spread[dy, pl.ds(5 + seg * SEG + dy, rows), :]
        if dy == 0:
            moved = jnp.where(even, 0.0, moved)
        if dy == 6:
            moved = jnp.where(even, moved, 0.0)
        total = moved if total is None else total + moved
    return total


def put(spread, fine, coarse):
    for seg in range(fine.shape[0] // NY):
        spread[pl.ds(8 + seg * SEG, NY), :] = fine[seg * NY : (seg + 1) * NY]
    spread[pl.ds(8 + (fine.shape[0] // NY) * SEG, HY), :] = coarse


def finish(fine_ref, done, px, pz):
    for child in range(4):
        first = (2 * px + child // 2) * 4 + 2 * pz + child % 2
        fine_ref[pl.ds(first, COEF, stride=16), :] = done[child * SLOT : child * SLOT + COEF]


def inner_kernel(out_ref, in_ref, pair_ref, tables, part_ref, sums_ref, sources, beyond, spread, rows):
    core = core_parity()
    sign = 1 - 2 * core
    clear_gaps(spread, 4)
    for at, ref in enumerate((out_ref, in_ref, pair_ref)):
        fine, coarse = sources_of(ref, rows.at[at])
        if at < 2:
            sources[pl.ds(256 * at, 256), :] = fine
            sources[pl.ds(512, HY), :] = coarse
        else:
            beyond[pl.ds(0, 256), :] = fine
            beyond[pl.ds(256, HY), :] = coarse
    for dy in range(7):
        if 2 <= dy <= 4:
            beside = jnp.concatenate([sources[:, 0:256], sources[:, 512:768]], axis=1)
            same = dot(beside, operator(tables, dy, 1, True))
        else:
            same = dot(sources[...], operator(tables, dy, 1))
        ahead = dot(jnp.concatenate([sources[256:512, :], beyond[...]], axis=0), operator(tables, dy, 1 + sign))
        behind = dot(sources[0:256, :], operator(tables, dy, 1 - sign))
        to_out = same[0:256] + ahead[0:256]
        to_in = same[256:512] + ahead[256:512] + behind
        put(spread.at[dy], jnp.concatenate([to_out, to_in], axis=0), same[512:] + ahead[512:])
    for seg in range(2):
        sums_ref[pl.ds(seg * NY, NY), :] = shifted(spread, seg, NY)
        finish(part_ref, shifted(spread, 2 + seg, NY).T, seg, 1 - core)
    sums_ref[pl.ds(2 * NY, HY), :] = shifted(spread, 4, HY)


def inner(out, into, pair, tables):
    vmem = pl.BlockSpec(memory_space=pltpu.VMEM)
    return pl.pallas_call(
        inner_kernel,
        in_specs=[vmem] * 4,
        out_specs=[vmem] * 2,
        out_shape=[
            jax.ShapeDtypeStruct((16 * COEF, NY), F32),
            jax.ShapeDtypeStruct((2 * NY + HY, 256), F32),
        ],
        scratch_shapes=[
            pltpu.VMEM((4 * NY + HY, 768), BF16),
            pltpu.VMEM((2 * NY + HY, 768), BF16),
            pltpu.VMEM((7, 4 * SEG + HY + 16, 256), F32),
            pltpu.VMEM((3, ROWS + 16, NY), F32),
        ],
        compiler_params=pltpu.CompilerParams(vmem_limit_bytes=VMEM),
        cost_estimate=pl.CostEstimate(flops=3_000_000_000, bytes_accessed=6_000_000, transcendentals=0),
        name="inner",
    )(out, into, pair, pltpu.with_memory_space_constraint(tables, pltpu.VMEM))


def outer_kernel(cross_ref, tables, part_ref, sums_ref, fine_ref, coarse_ref, sources, spread, shuffled, rows):
    core = core_parity()
    clear_gaps(spread, 2)
    sources[...] = jnp.concatenate(sources_of(cross_ref, rows), axis=0)
    for dy in range(7):
        found = dot(sources[...], operator(tables, dy, 2 * core))
        put(spread.at[dy], found[0:256], found[256:])
    fine_ref[...] = part_ref[...]
    for seg in range(2):
        finish(fine_ref, (sums_ref[pl.ds(seg * NY, NY), :] + shifted(spread, seg, NY)).T, seg, core)
    done = (sums_ref[pl.ds(2 * NY, HY), :] + shifted(spread, 2, HY)).T
    for child in range(4):
        shuffled[pl.ds(child, COEF, stride=4), :] = done[child * SLOT : child * SLOT + COEF]
    coarse_ref[...] = shuffled[...].reshape(COEF, 2, 2, HY)


def outer(cross, tables, part, sums):
    vmem = pl.BlockSpec(memory_space=pltpu.VMEM)
    return pl.pallas_call(
        outer_kernel,
        in_specs=[vmem] * 4,
        out_specs=[vmem, vmem],
        out_shape=[
            jax.ShapeDtypeStruct((16 * COEF, NY), F32),
            jax.ShapeDtypeStruct((COEF, 2, 2, HY), F32),
        ],
        scratch_shapes=[
            pltpu.VMEM((2 * NY + HY, 768), BF16),
            pltpu.VMEM((7, 2 * SEG + HY + 16, 256), F32),
            pltpu.VMEM((4 * COEF, HY), F32),
            pltpu.VMEM((ROWS + 16, NY), F32),
        ],
        compiler_params=pltpu.CompilerParams(vmem_limit_bytes=VMEM),
        cost_estimate=pl.CostEstimate(flops=1_000_000_000, bytes_accessed=5_000_000, transcendentals=0),
        name="outer",
    )(cross, pltpu.with_memory_space_constraint(tables, pltpu.VMEM), part, sums)


def exchange(array, axis, start):
    count = lax.axis_size(axis)
    there = [(i, i + 1) for i in range(start, count - 1, 2)]
    return lax.ppermute(array, axis, there + [(j, i) for i, j in there])


def shards(multipoles, translate_far, translate_up):
    up = translate_up.transpose(1, 0, 2).reshape(8 * COEF, COEF)
    to_a, to_b, packed, coarse = own_part(multipoles.reshape(16 * COEF, NY), up)
    b = exchange(to_b, "wide", 1)
    a = exchange(to_a, "wide", 0)
    tables, parents = make_tables(translate_far, coarse)
    out, into = pack(b, a, packed, to_b, tables)
    pair = exchange(into, "narrow", 0)
    cross = exchange(out, "narrow", 1)
    part, sums = inner(out, into, pair, tables)
    fine, coarse_locals = outer(cross, tables, part, sums)
    return fine.reshape(COEF, 4, 4, NY), parents, coarse_locals


def solution(mesh):
    return jax.shard_map(
        shards,
        mesh=mesh,
        in_specs=(P(None, "wide", "narrow", None), P(), P()),
        out_specs=(
            P(None, "wide", "narrow", None),
            P(None, "wide", "narrow", None),
            P(None, "wide", "narrow", None),
        ),
        check_vma=False,
    )
```

```python
import jax
import jax.numpy as jnp
from jax import lax
from jax.experimental import pallas as pl
from jax.experimental.pallas import tpu as pltpu
from jax.sharding import PartitionSpec as P

F32 = jnp.float32
BF16 = jnp.bfloat16
NT = (((1,), (1,)), ((), ()))
COEF = 49
SLOT = 64
NY = 128
HY = 64
BLOCK = 208
PAIR = 112
SIDE = 2 * BLOCK + PAIR
COLUMN = 4 * BLOCK
ROWS = COLUMN + 3 * PAIR
SEG = NY + 8
VMEM = 20 * 2**20


def dot(a, b):
    return jnp.dot(a, b, preferred_element_type=F32)


def eye(n):
    rows = lax.broadcasted_iota(jnp.int32, (n, n), 0)
    cols = lax.broadcasted_iota(jnp.int32, (n, n), 1)
    return jnp.where(rows == cols, 1.0, 0.0).astype(BF16)


def core_parity():
    return lax.rem(lax.axis_index("narrow"), 2)


def turn(unit, cells):
    return lax.dot_general(unit, cells.astype(BF16), NT, preferred_element_type=F32)


def own_kernel(
    own_hbm, up_hbm, a_ref, b_ref, packed_ref, coarse_ref,
    own, up, brick, packed, wide, pairs, parents_t, sems,
):
    odd = lax.rem(lax.axis_index("wide"), 2)
    get_up = pltpu.make_async_copy(up_hbm, up, sems.at[0])
    get_own = pltpu.make_async_copy(own_hbm, own, sems.at[1])
    get_own.start()
    get_up.start()
    pairs[...] = jnp.zeros_like(pairs)
    brick[pl.ds(16 * COEF, 16 * (SLOT - COEF)), :] = jnp.zeros((16 * (SLOT - COEF), NY), F32)
    get_own.wait()
    get_up.wait()
    wide[...] = up[...].astype(F32)
    for child in range(8):
        block = wide[pl.ds(child, COEF, stride=8), :].astype(BF16)
        pairs[pl.ds(SLOT * (child // 2), COEF), pl.ds(SLOT * (child % 2), COEF)] = block
    pairs_t = pairs[...].T
    brick[pl.ds(0, 16 * COEF), :] = own[...].astype(F32)
    cells = [brick[pl.ds(cell, SLOT, stride=16), :] for cell in range(16)]
    order = [(2 * px + cx) * 4 + 2 * zp + cz for px in range(2) for zp in range(2) for cx in range(2) for cz in range(2)]
    for at, cell in enumerate(order):
        packed[pl.ds(BLOCK * (at // 4) + COEF * (at % 4), SLOT), :] = cells[cell]
    packed_ref[...] = packed[pl.ds(0, COLUMN), :].astype(BF16)
    a_ref[pl.ds(0, 2 * BLOCK), :] = packed_ref[pl.ds(pl.multiple_of((1 - odd) * 2 * BLOCK, 16), 2 * BLOCK), :]
    b_ref[pl.ds(0, 2 * BLOCK), :] = packed_ref[pl.ds(pl.multiple_of(odd * 2 * BLOCK, 16), 2 * BLOCK), :]
    lane = lax.broadcasted_iota(jnp.int32, (SLOT, NY), 1)
    even = 2 * lax.rem(lane, HY)
    for zp in range(2):
        found = []
        for px in range(2):
            part = jnp.concatenate([cells[cell] for cell in order[8 * px + 4 * zp : 8 * px + 4 * zp + 4]], axis=0)
            both = dot(pairs_t, part.astype(BF16))
            first = jnp.take_along_axis(both[0:SLOT], even, axis=1, mode="promise_in_bounds")
            second = jnp.take_along_axis(both[SLOT:128], even + 1, axis=1, mode="promise_in_bounds")
            found.append(first + second)
        parents = jnp.where(lane < HY, found[0], found[1])
        parents_t[pl.ds(COEF * zp, SLOT), :] = parents
        coarse_ref[pl.ds(SLOT * zp, SLOT), :] = parents.astype(BF16)
    for ref in (a_ref, b_ref):
        ref[pl.ds(2 * BLOCK, PAIR), :] = parents_t[pl.ds(0, PAIR), :].astype(BF16)


def own_part(own, up):
    hbm = pl.BlockSpec(memory_space=pltpu.HBM)
    vmem = pl.BlockSpec(memory_space=pltpu.VMEM)
    return pl.pallas_call(
        own_kernel,
        in_specs=[hbm] * 2,
        out_specs=[vmem] * 4,
        out_shape=[
            pltpu.VMEM((SIDE, NY), BF16),
            pltpu.VMEM((SIDE, NY), BF16),
            pltpu.VMEM((COLUMN, NY), BF16),
            pltpu.VMEM((128, 128), BF16),
        ],
        scratch_shapes=[
            pltpu.VMEM((16 * COEF, NY), BF16),
            pltpu.VMEM((8 * COEF, COEF), BF16),
            pltpu.VMEM((16 * SLOT, NY), F32),
            pltpu.VMEM((COLUMN + 16, NY), F32),
            pltpu.VMEM((8 * COEF, COEF), F32),
            pltpu.VMEM((256, 128), BF16),
            pltpu.VMEM((120, NY), F32),
            pltpu.SemaphoreType.DMA((2,)),
        ],
        compiler_params=pltpu.CompilerParams(vmem_limit_bytes=VMEM),
        name="own_part",
    )(*[pltpu.with_memory_space_constraint(x, pltpu.HBM) for x in (own, up)])


def tables_kernel(far_hbm, coarse_ref, tables_ref, par_ref, far, shuffled, sems):
    def fetch(dx):
        return pltpu.make_async_copy(far_hbm.at[dx], far.at[dx], sems.at[dx])

    for dx in range(2):
        fetch(dx).start()

    turned = coarse_ref[...].astype(F32)
    for px in range(2):
        for z in range(2):
            block = turned[z * SLOT : z * SLOT + COEF, px * HY : (px + 1) * HY]
            shuffled[pl.ds(2 * px + z, COEF, stride=4), :] = block
    par_ref[...] = shuffled[...].astype(BF16).reshape(COEF, 2, 2, HY)

    def at_dx(dx, carry):
        fetch(dx).wait()

        @pl.when(dx < 5)
        def _():
            fetch(dx + 2).start()

        keep = jnp.where(jnp.abs(dx - 3) <= 1, 0.0, 1.0).astype(BF16)
        for dy in range(7):
            left, right = [], []
            for dz in range(7):
                block = far[dx, dz, dy]
                if abs(dz - 3) <= 1 and abs(dy - 3) <= 1:
                    block = block * keep
                block = jnp.pad(block, ((0, SLOT - COEF), (0, 128 - COEF)))
                left.append(block)
                right.append(jnp.concatenate([block[:, SLOT:], block[:, :SLOT]], axis=1))
            for sz in range(3):
                for cz in range(2):
                    tables_ref[dy, sz, dx, pl.ds(SLOT * cz, SLOT), :] = left[2 * sz + 1 + cz] + right[2 * sz + cz]
        return carry

    lax.fori_loop(0, 7, at_dx, 0)


def make_tables(far, coarse):
    vmem = pl.BlockSpec(memory_space=pltpu.VMEM)
    return pl.pallas_call(
        tables_kernel,
        in_specs=[pl.BlockSpec(memory_space=pltpu.HBM), vmem],
        out_specs=[vmem] * 2,
        out_shape=[
            pltpu.VMEM((7, 3, 7, 128, 128), BF16),
            jax.ShapeDtypeStruct((COEF, 2, 2, HY), BF16),
        ],
        scratch_shapes=[
            pltpu.VMEM((7, 7, 7, COEF, COEF), BF16),
            pltpu.VMEM((4 * COEF, HY), F32),
            pltpu.SemaphoreType.DMA((7,)),
        ],
        compiler_params=pltpu.CompilerParams(vmem_limit_bytes=VMEM),
        cost_estimate=pl.CostEstimate(flops=0, bytes_accessed=10_000_000, transcendentals=0),
        name="tables",
    )(pltpu.with_memory_space_constraint(far, pltpu.HBM), pltpu.with_memory_space_constraint(coarse, pltpu.VMEM))


def pack_kernel(b_ref, a_ref, packed_ref, mine_ref, tables_ref, out_ref, in_ref):
    odd, core = lax.rem(lax.axis_index("wide"), 2), core_parity()
    for q, ref in enumerate((out_ref, in_ref)):
        zp = q + core - 2 * q * core
        for px in range(2):
            row = pl.multiple_of((2 * px + zp) * BLOCK, 16)
            ref[pl.ds((1 + px) * BLOCK, BLOCK), :] = packed_ref[pl.ds(row, BLOCK), :]
        ref[pl.ds(COLUMN + PAIR, PAIR), :] = mine_ref[pl.ds(2 * BLOCK, PAIR), :]
        for side, above in ((b_ref, odd), (a_ref, 1 - odd)):
            row = pl.multiple_of(above * 3 * BLOCK, 16)
            ref[pl.ds(row, BLOCK), :] = side[pl.ds(pl.multiple_of(zp * BLOCK, 16), BLOCK), :]
            row = pl.multiple_of(COLUMN + above * 2 * PAIR, 16)
            ref[pl.ds(row, PAIR), :] = side[pl.ds(2 * BLOCK, PAIR), :]


def pack(b, a, packed, mine, tables):
    vmem = pl.BlockSpec(memory_space=pltpu.VMEM)
    return pl.pallas_call(
        pack_kernel,
        in_specs=[vmem] * 5,
        out_specs=[vmem] * 2,
        out_shape=[jax.ShapeDtypeStruct((ROWS, NY), BF16)] * 2,
        compiler_params=pltpu.CompilerParams(vmem_limit_bytes=VMEM),
        name="pack",
    )(b, a, *[pltpu.with_memory_space_constraint(x, pltpu.VMEM) for x in (packed, mine, tables)])


def operator(tables, dy, at, skip=False):
    blocks = [tables[dy, at, dx] for dx in range(7)]
    return jnp.concatenate(
        [jnp.concatenate([blocks[e + 1], blocks[e]], axis=1) for e in range(6) if not (skip and e in (2, 3))],
        axis=0,
    )


def sources_of(ref, rows):
    rows[pl.ds(0, ROWS), :] = ref[...].astype(F32)
    rows[pl.ds(ROWS, 16), :] = jnp.zeros((16, NY), F32)
    cells = [rows[pl.ds(BLOCK * at + COEF * cell, SLOT), :] for at in range(4) for cell in range(4)]
    cells += [rows[pl.ds(COLUMN + PAIR * at + COEF * z, SLOT), :] for at in range(3) for z in range(2)]
    turned = turn(eye(NY), jnp.concatenate(cells, axis=0)).astype(BF16)
    fine = jnp.concatenate([turned[:, 0:768], turned[:, 256:1024]], axis=0)
    parts = [turned[px * HY : (px + 1) * HY, 1024 + 128 * at : 1152 + 128 * at] for at in range(3) for px in range(2)]
    return fine, jnp.concatenate(parts, axis=1)


def clear_gaps(spread, count):
    for seg in range(count + 1):
        spread[:, pl.ds(seg * SEG, 8), :] = jnp.zeros((7, 8, 256), F32)
    spread[:, pl.ds(8 + count * SEG + HY, 8), :] = jnp.zeros((7, 8, 256), F32)


def shifted(spread, seg, rows):
    even = lax.broadcasted_iota(jnp.int32, (rows, 256), 0) % 2 == 0
    total = None
    for dy in range(7):
        moved = spread[dy, pl.ds(5 + seg * SEG + dy, rows), :]
        if dy == 0:
            moved = jnp.where(even, 0.0, moved)
        if dy == 6:
            moved = jnp.where(even, moved, 0.0)
        total = moved if total is None else total + moved
    return total


def put(spread, fine, coarse):
    for seg in range(fine.shape[0] // NY):
        spread[pl.ds(8 + seg * SEG, NY), :] = fine[seg * NY : (seg + 1) * NY]
    spread[pl.ds(8 + (fine.shape[0] // NY) * SEG, HY), :] = coarse


def finish(fine_ref, done, px, pz):
    for child in range(4):
        first = (2 * px + child // 2) * 4 + 2 * pz + child % 2
        fine_ref[pl.ds(first, COEF, stride=16), :] = done[child * SLOT : child * SLOT + COEF]


def inner_kernel(out_ref, in_ref, pair_ref, tables, part_ref, sums_ref, sources, beyond, spread, rows):
    core = core_parity()
    sign = 1 - 2 * core
    clear_gaps(spread, 4)
    for at, ref in enumerate((out_ref, in_ref, pair_ref)):
        fine, coarse = sources_of(ref, rows.at[at])
        if at < 2:
            sources[pl.ds(256 * at, 256), :] = fine
            sources[pl.ds(512, HY), :] = coarse
        else:
            beyond[pl.ds(0, 256), :] = fine
            beyond[pl.ds(256, HY), :] = coarse
    for dy in range(7):
        if 2 <= dy <= 4:
            beside = jnp.concatenate([sources[:, 0:256], sources[:, 512:768]], axis=1)
            same = dot(beside, operator(tables, dy, 1, True))
        else:
            same = dot(sources[...], operator(tables, dy, 1))
        ahead = dot(jnp.concatenate([sources[256:512, :], beyond[...]], axis=0), operator(tables, dy, 1 + sign))
        behind = dot(sources[0:256, :], operator(tables, dy, 1 - sign))
        to_out = same[0:256] + ahead[0:256]
        to_in = same[256:512] + ahead[256:512] + behind
        put(spread.at[dy], jnp.concatenate([to_out, to_in], axis=0), same[512:] + ahead[512:])
    for seg in range(2):
        sums_ref[pl.ds(seg * NY, NY), :] = shifted(spread, seg, NY)
        finish(part_ref, shifted(spread, 2 + seg, NY).T, seg, 1 - core)
    sums_ref[pl.ds(2 * NY, HY), :] = shifted(spread, 4, HY)


def inner(out, into, pair, tables):
    vmem = pl.BlockSpec(memory_space=pltpu.VMEM)
    return pl.pallas_call(
        inner_kernel,
        in_specs=[vmem] * 4,
        out_specs=[vmem] * 2,
        out_shape=[
            jax.ShapeDtypeStruct((16 * COEF, NY), F32),
            jax.ShapeDtypeStruct((2 * NY + HY, 256), F32),
        ],
        scratch_shapes=[
            pltpu.VMEM((4 * NY + HY, 768), BF16),
            pltpu.VMEM((2 * NY + HY, 768), BF16),
            pltpu.VMEM((7, 4 * SEG + HY + 16, 256), F32),
            pltpu.VMEM((3, ROWS + 16, NY), F32),
        ],
        compiler_params=pltpu.CompilerParams(vmem_limit_bytes=VMEM),
        cost_estimate=pl.CostEstimate(flops=3_000_000_000, bytes_accessed=6_000_000, transcendentals=0),
        name="inner",
    )(out, into, pair, pltpu.with_memory_space_constraint(tables, pltpu.VMEM))


def outer_kernel(cross_ref, tables, part_ref, sums_ref, fine_ref, coarse_ref, sources, spread, shuffled, rows):
    core = core_parity()
    clear_gaps(spread, 2)
    sources[...] = jnp.concatenate(sources_of(cross_ref, rows), axis=0)
    for dy in range(7):
        found = dot(sources[...], operator(tables, dy, 2 * core))
        put(spread.at[dy], found[0:256], found[256:])
    fine_ref[...] = part_ref[...]
    for seg in range(2):
        finish(fine_ref, (sums_ref[pl.ds(seg * NY, NY), :] + shifted(spread, seg, NY)).T, seg, core)
    done = (sums_ref[pl.ds(2 * NY, HY), :] + shifted(spread, 2, HY)).T
    for child in range(4):
        shuffled[pl.ds(child, COEF, stride=4), :] = done[child * SLOT : child * SLOT + COEF]
    coarse_ref[...] = shuffled[...].reshape(COEF, 2, 2, HY)


def outer(cross, tables, part, sums):
    vmem = pl.BlockSpec(memory_space=pltpu.VMEM)
    return pl.pallas_call(
        outer_kernel,
        in_specs=[vmem] * 4,
        out_specs=[vmem, vmem],
        out_shape=[
            jax.ShapeDtypeStruct((16 * COEF, NY), F32),
            jax.ShapeDtypeStruct((COEF, 2, 2, HY), F32),
        ],
        scratch_shapes=[
            pltpu.VMEM((2 * NY + HY, 768), BF16),
            pltpu.VMEM((7, 2 * SEG + HY + 16, 256), F32),
            pltpu.VMEM((4 * COEF, HY), F32),
            pltpu.VMEM((ROWS + 16, NY), F32),
        ],
        compiler_params=pltpu.CompilerParams(vmem_limit_bytes=VMEM),
        cost_estimate=pl.CostEstimate(flops=1_000_000_000, bytes_accessed=5_000_000, transcendentals=0),
        name="outer",
    )(cross, pltpu.with_memory_space_constraint(tables, pltpu.VMEM), part, sums)


def exchange(array, axis, start):
    count = lax.axis_size(axis)
    there = [(i, i + 1) for i in range(start, count - 1, 2)]
    return lax.ppermute(array, axis, there + [(j, i) for i, j in there])


def shards(multipoles, translate_far, translate_up):
    up = translate_up.transpose(1, 0, 2).reshape(8 * COEF, COEF)
    to_a, to_b, packed, coarse = own_part(multipoles.reshape(16 * COEF, NY), up)
    b = exchange(to_b, "wide", 1)
    a = exchange(to_a, "wide", 0)
    tables, parents = make_tables(translate_far, coarse)
    out, into = pack(b, a, packed, to_b, tables)
    pair = exchange(into, "narrow", 0)
    cross = exchange(out, "narrow", 1)
    part, sums = inner(out, into, pair, tables)
    fine, coarse_locals = outer(cross, tables, part, sums)
    return fine.reshape(COEF, 4, 4, NY), parents, coarse_locals


def solution(mesh):
    return jax.shard_map(
        shards,
        mesh=mesh,
        in_specs=(P(None, "wide", "narrow", None), P(), P()),
        out_specs=(
            P(None, "wide", "narrow", None),
            P(None, "wide", "narrow", None),
            P(None, "wide", "narrow", None),
        ),
        check_vma=False,
    )
```

```python
import jax
import jax.numpy as jnp
from jax import lax
from jax.experimental import pallas as pl
from jax.experimental.pallas import tpu as pltpu
from jax.sharding import PartitionSpec as P

F32 = jnp.float32
BF16 = jnp.bfloat16
NT = (((1,), (1,)), ((), ()))
COEF = 49
SLOT = 64
NY = 128
HY = 64
BLOCK = 208
PAIR = 112
SIDE = 2 * BLOCK + PAIR
COLUMN = 4 * BLOCK
ROWS = COLUMN + 3 * PAIR
SEG = NY + 8
VMEM = 20 * 2**20


def dot(a, b):
    return jnp.dot(a, b, preferred_element_type=F32)


def eye(n):
    rows = lax.broadcasted_iota(jnp.int32, (n, n), 0)
    cols = lax.broadcasted_iota(jnp.int32, (n, n), 1)
    return jnp.where(rows == cols, 1.0, 0.0).astype(BF16)


def core_parity():
    return lax.rem(lax.axis_index("narrow"), 2)


def turn(unit, cells):
    return lax.dot_general(unit, cells.astype(BF16), NT, preferred_element_type=F32)


def own_kernel(
    own_hbm, up_hbm, a_ref, b_ref, packed_ref, coarse_ref,
    own, up, brick, packed, wide, pairs, parents_t, sems,
):
    odd = lax.rem(lax.axis_index("wide"), 2)
    get_up = pltpu.make_async_copy(up_hbm, up, sems.at[0])
    get_own = pltpu.make_async_copy(own_hbm, own, sems.at[1])
    get_own.start()
    get_up.start()
    pairs[...] = jnp.zeros_like(pairs)
    brick[pl.ds(16 * COEF, 16 * (SLOT - COEF)), :] = jnp.zeros((16 * (SLOT - COEF), NY), F32)
    get_own.wait()
    get_up.wait()
    wide[...] = up[...].astype(F32)
    for child in range(8):
        block = wide[pl.ds(child, COEF, stride=8), :].astype(BF16)
        pairs[pl.ds(SLOT * (child // 2), COEF), pl.ds(SLOT * (child % 2), COEF)] = block
    pairs_t = pairs[...].T
    brick[pl.ds(0, 16 * COEF), :] = own[...].astype(F32)
    cells = [brick[pl.ds(cell, SLOT, stride=16), :] for cell in range(16)]
    order = [(2 * px + cx) * 4 + 2 * zp + cz for px in range(2) for zp in range(2) for cx in range(2) for cz in range(2)]
    for at, cell in enumerate(order):
        packed[pl.ds(BLOCK * (at // 4) + COEF * (at % 4), SLOT), :] = cells[cell]
    packed_ref[...] = packed[pl.ds(0, COLUMN), :].astype(BF16)
    a_ref[pl.ds(0, 2 * BLOCK), :] = packed_ref[pl.ds(pl.multiple_of((1 - odd) * 2 * BLOCK, 16), 2 * BLOCK), :]
    b_ref[pl.ds(0, 2 * BLOCK), :] = packed_ref[pl.ds(pl.multiple_of(odd * 2 * BLOCK, 16), 2 * BLOCK), :]
    lane = lax.broadcasted_iota(jnp.int32, (SLOT, NY), 1)
    even = 2 * lax.rem(lane, HY)
    every = jnp.concatenate(
        [jnp.concatenate([cells[cell] for cell in order[4 * at : 4 * at + 4]], axis=0).astype(BF16) for at in range(4)],
        axis=1,
    )
    product = dot(pairs_t, every)
    for zp in range(2):
        found = []
        for px in range(2):
            both = product[:, (2 * px + zp) * NY : (2 * px + zp + 1) * NY]
            first = jnp.take_along_axis(both[0:SLOT], even, axis=1, mode="promise_in_bounds")
            second = jnp.take_along_axis(both[SLOT:128], even + 1, axis=1, mode="promise_in_bounds")
            found.append(first + second)
        parents = jnp.where(lane < HY, found[0], found[1])
        parents_t[pl.ds(COEF * zp, SLOT), :] = parents
        coarse_ref[pl.ds(SLOT * zp, SLOT), :] = parents.astype(BF16)
    for ref in (a_ref, b_ref):
        ref[pl.ds(2 * BLOCK, PAIR), :] = parents_t[pl.ds(0, PAIR), :].astype(BF16)


def own_part(own, up):
    hbm = pl.BlockSpec(memory_space=pltpu.HBM)
    vmem = pl.BlockSpec(memory_space=pltpu.VMEM)
    return pl.pallas_call(
        own_kernel,
        in_specs=[hbm] * 2,
        out_specs=[vmem] * 4,
        out_shape=[
            pltpu.VMEM((SIDE, NY), BF16),
            pltpu.VMEM((SIDE, NY), BF16),
            pltpu.VMEM((COLUMN, NY), BF16),
            pltpu.VMEM((128, 128), BF16),
        ],
        scratch_shapes=[
            pltpu.VMEM((16 * COEF, NY), BF16),
            pltpu.VMEM((8 * COEF, COEF), BF16),
            pltpu.VMEM((16 * SLOT, NY), F32),
            pltpu.VMEM((COLUMN + 16, NY), F32),
            pltpu.VMEM((8 * COEF, COEF), F32),
            pltpu.VMEM((256, 128), BF16),
            pltpu.VMEM((120, NY), F32),
            pltpu.SemaphoreType.DMA((2,)),
        ],
        compiler_params=pltpu.CompilerParams(vmem_limit_bytes=VMEM),
        name="own_part",
    )(*[pltpu.with_memory_space_constraint(x, pltpu.HBM) for x in (own, up)])


def tables_kernel(far_hbm, coarse_ref, tables_ref, par_ref, far, shuffled, sems):
    def fetch(dx):
        return pltpu.make_async_copy(far_hbm.at[dx], far.at[dx], sems.at[dx])

    for dx in range(7):
        fetch(dx).start()

    turned = coarse_ref[...].astype(F32)
    for px in range(2):
        for z in range(2):
            block = turned[z * SLOT : z * SLOT + COEF, px * HY : (px + 1) * HY]
            shuffled[pl.ds(2 * px + z, COEF, stride=4), :] = block
    par_ref[...] = shuffled[...].astype(BF16).reshape(COEF, 2, 2, HY)

    def at_dx(dx, carry):
        fetch(dx).wait()
        keep = jnp.where(jnp.abs(dx - 3) <= 1, 0.0, 1.0).astype(BF16)
        for dy in range(7):
            left, right = [], []
            for dz in range(7):
                block = far[dx, dz, dy]
                if abs(dz - 3) <= 1 and abs(dy - 3) <= 1:
                    block = block * keep
                block = jnp.pad(block, ((0, SLOT - COEF), (0, 128 - COEF)))
                left.append(block)
                right.append(jnp.concatenate([block[:, SLOT:], block[:, :SLOT]], axis=1))
            for sz in range(3):
                for cz in range(2):
                    tables_ref[dy, sz, dx, pl.ds(SLOT * cz, SLOT), :] = left[2 * sz + 1 + cz] + right[2 * sz + cz]
        return carry

    lax.fori_loop(0, 7, at_dx, 0)


def make_tables(far, coarse):
    vmem = pl.BlockSpec(memory_space=pltpu.VMEM)
    return pl.pallas_call(
        tables_kernel,
        in_specs=[pl.BlockSpec(memory_space=pltpu.HBM), vmem],
        out_specs=[vmem] * 2,
        out_shape=[
            pltpu.VMEM((7, 3, 7, 128, 128), BF16),
            jax.ShapeDtypeStruct((COEF, 2, 2, HY), BF16),
        ],
        scratch_shapes=[
            pltpu.VMEM((7, 7, 7, COEF, COEF), BF16),
            pltpu.VMEM((4 * COEF, HY), F32),
            pltpu.SemaphoreType.DMA((7,)),
        ],
        compiler_params=pltpu.CompilerParams(vmem_limit_bytes=VMEM),
        cost_estimate=pl.CostEstimate(flops=0, bytes_accessed=10_000_000, transcendentals=0),
        name="tables",
    )(pltpu.with_memory_space_constraint(far, pltpu.HBM), pltpu.with_memory_space_constraint(coarse, pltpu.VMEM))


def pack_kernel(b_ref, a_ref, packed_ref, mine_ref, tables_ref, out_ref, in_ref):
    odd, core = lax.rem(lax.axis_index("wide"), 2), core_parity()
    for q, ref in enumerate((out_ref, in_ref)):
        zp = q + core - 2 * q * core
        for px in range(2):
            row = pl.multiple_of((2 * px + zp) * BLOCK, 16)
            ref[pl.ds((1 + px) * BLOCK, BLOCK), :] = packed_ref[pl.ds(row, BLOCK), :]
        ref[pl.ds(COLUMN + PAIR, PAIR), :] = mine_ref[pl.ds(2 * BLOCK, PAIR), :]
        for side, above in ((b_ref, odd), (a_ref, 1 - odd)):
            row = pl.multiple_of(above * 3 * BLOCK, 16)
            ref[pl.ds(row, BLOCK), :] = side[pl.ds(pl.multiple_of(zp * BLOCK, 16), BLOCK), :]
            row = pl.multiple_of(COLUMN + above * 2 * PAIR, 16)
            ref[pl.ds(row, PAIR), :] = side[pl.ds(2 * BLOCK, PAIR), :]


def pack(b, a, packed, mine, tables):
    vmem = pl.BlockSpec(memory_space=pltpu.VMEM)
    return pl.pallas_call(
        pack_kernel,
        in_specs=[vmem] * 5,
        out_specs=[vmem] * 2,
        out_shape=[jax.ShapeDtypeStruct((ROWS, NY), BF16)] * 2,
        compiler_params=pltpu.CompilerParams(vmem_limit_bytes=VMEM),
        name="pack",
    )(b, a, *[pltpu.with_memory_space_constraint(x, pltpu.VMEM) for x in (packed, mine, tables)])


def operator(tables, dy, at, skip=False):
    blocks = [tables[dy, at, dx] for dx in range(7)]
    return jnp.concatenate(
        [jnp.concatenate([blocks[e + 1], blocks[e]], axis=1) for e in range(6) if not (skip and e in (2, 3))],
        axis=0,
    )


def sources_of(ref, rows):
    rows[pl.ds(0, ROWS), :] = ref[...].astype(F32)
    rows[pl.ds(ROWS, 16), :] = jnp.zeros((16, NY), F32)
    cells = [rows[pl.ds(BLOCK * at + COEF * cell, SLOT), :] for at in range(4) for cell in range(4)]
    cells += [rows[pl.ds(COLUMN + PAIR * at + COEF * z, SLOT), :] for at in range(3) for z in range(2)]
    turned = turn(eye(NY), jnp.concatenate(cells, axis=0)).astype(BF16)
    fine = jnp.concatenate([turned[:, 0:768], turned[:, 256:1024]], axis=0)
    parts = [turned[px * HY : (px + 1) * HY, 1024 + 128 * at : 1152 + 128 * at] for at in range(3) for px in range(2)]
    return fine, jnp.concatenate(parts, axis=1)


def clear_gaps(spread, count):
    for seg in range(count + 1):
        spread[:, pl.ds(seg * SEG, 8), :] = jnp.zeros((7, 8, 256), F32)
    spread[:, pl.ds(8 + count * SEG + HY, 8), :] = jnp.zeros((7, 8, 256), F32)


def shifted(spread, seg, rows):
    even = lax.broadcasted_iota(jnp.int32, (rows, 256), 0) % 2 == 0
    total = None
    for dy in range(7):
        moved = spread[dy, pl.ds(5 + seg * SEG + dy, rows), :]
        if dy == 0:
            moved = jnp.where(even, 0.0, moved)
        if dy == 6:
            moved = jnp.where(even, moved, 0.0)
        total = moved if total is None else total + moved
    return total


def put(spread, fine, coarse):
    for seg in range(fine.shape[0] // NY):
        spread[pl.ds(8 + seg * SEG, NY), :] = fine[seg * NY : (seg + 1) * NY]
    spread[pl.ds(8 + (fine.shape[0] // NY) * SEG, HY), :] = coarse


def finish(fine_ref, done, px, pz):
    for child in range(4):
        first = (2 * px + child // 2) * 4 + 2 * pz + child % 2
        fine_ref[pl.ds(first, COEF, stride=16), :] = done[child * SLOT : child * SLOT + COEF]


def inner_kernel(out_ref, in_ref, pair_ref, tables, part_ref, sums_ref, sources, beyond, spread, rows):
    core = core_parity()
    sign = 1 - 2 * core
    clear_gaps(spread, 4)
    for at, ref in enumerate((out_ref, in_ref, pair_ref)):
        fine, coarse = sources_of(ref, rows.at[at])
        if at < 2:
            sources[pl.ds(256 * at, 256), :] = fine
            sources[pl.ds(512, HY), :] = coarse
        else:
            beyond[pl.ds(0, 256), :] = fine
            beyond[pl.ds(256, HY), :] = coarse
    for dy in range(7):
        if 2 <= dy <= 4:
            beside = jnp.concatenate([sources[:, 0:256], sources[:, 512:768]], axis=1)
            same = dot(beside, operator(tables, dy, 1, True))
        else:
            same = dot(sources[...], operator(tables, dy, 1))
        ahead = dot(jnp.concatenate([sources[256:512, :], beyond[...]], axis=0), operator(tables, dy, 1 + sign))
        behind = dot(sources[0:256, :], operator(tables, dy, 1 - sign))
        to_out = same[0:256] + ahead[0:256]
        to_in = same[256:512] + ahead[256:512] + behind
        put(spread.at[dy], jnp.concatenate([to_out, to_in], axis=0), same[512:] + ahead[512:])
    for seg in range(2):
        sums_ref[pl.ds(seg * NY, NY), :] = shifted(spread, seg, NY)
        finish(part_ref, shifted(spread, 2 + seg, NY).T, seg, 1 - core)
    sums_ref[pl.ds(2 * NY, HY), :] = shifted(spread, 4, HY)


def inner(out, into, pair, tables):
    vmem = pl.BlockSpec(memory_space=pltpu.VMEM)
    return pl.pallas_call(
        inner_kernel,
        in_specs=[vmem] * 4,
        out_specs=[vmem] * 2,
        out_shape=[
            jax.ShapeDtypeStruct((16 * COEF, NY), F32),
            jax.ShapeDtypeStruct((2 * NY + HY, 256), F32),
        ],
        scratch_shapes=[
            pltpu.VMEM((4 * NY + HY, 768), BF16),
            pltpu.VMEM((2 * NY + HY, 768), BF16),
            pltpu.VMEM((7, 4 * SEG + HY + 16, 256), F32),
            pltpu.VMEM((3, ROWS + 16, NY), F32),
        ],
        compiler_params=pltpu.CompilerParams(vmem_limit_bytes=VMEM),
        cost_estimate=pl.CostEstimate(flops=3_000_000_000, bytes_accessed=6_000_000, transcendentals=0),
        name="inner",
    )(out, into, pair, pltpu.with_memory_space_constraint(tables, pltpu.VMEM))


def outer_kernel(cross_ref, tables, part_ref, sums_ref, fine_ref, coarse_ref, sources, spread, shuffled, rows):
    core = core_parity()
    clear_gaps(spread, 2)
    sources[...] = jnp.concatenate(sources_of(cross_ref, rows), axis=0)
    for dy in range(7):
        found = dot(sources[...], operator(tables, dy, 2 * core))
        put(spread.at[dy], found[0:256], found[256:])
    fine_ref[...] = part_ref[...]
    for seg in range(2):
        finish(fine_ref, (sums_ref[pl.ds(seg * NY, NY), :] + shifted(spread, seg, NY)).T, seg, core)
    done = (sums_ref[pl.ds(2 * NY, HY), :] + shifted(spread, 2, HY)).T
    for child in range(4):
        shuffled[pl.ds(child, COEF, stride=4), :] = done[child * SLOT : child * SLOT + COEF]
    coarse_ref[...] = shuffled[...].reshape(COEF, 2, 2, HY)


def outer(cross, tables, part, sums):
    vmem = pl.BlockSpec(memory_space=pltpu.VMEM)
    return pl.pallas_call(
        outer_kernel,
        in_specs=[vmem] * 4,
        out_specs=[vmem, vmem],
        out_shape=[
            jax.ShapeDtypeStruct((16 * COEF, NY), F32),
            jax.ShapeDtypeStruct((COEF, 2, 2, HY), F32),
        ],
        scratch_shapes=[
            pltpu.VMEM((2 * NY + HY, 768), BF16),
            pltpu.VMEM((7, 2 * SEG + HY + 16, 256), F32),
            pltpu.VMEM((4 * COEF, HY), F32),
            pltpu.VMEM((ROWS + 16, NY), F32),
        ],
        compiler_params=pltpu.CompilerParams(vmem_limit_bytes=VMEM),
        cost_estimate=pl.CostEstimate(flops=1_000_000_000, bytes_accessed=5_000_000, transcendentals=0),
        name="outer",
    )(cross, pltpu.with_memory_space_constraint(tables, pltpu.VMEM), part, sums)


def exchange(array, axis, start):
    count = lax.axis_size(axis)
    there = [(i, i + 1) for i in range(start, count - 1, 2)]
    return lax.ppermute(array, axis, there + [(j, i) for i, j in there])


def shards(multipoles, translate_far, translate_up):
    up = translate_up.transpose(1, 0, 2).reshape(8 * COEF, COEF)
    to_a, to_b, packed, coarse = own_part(multipoles.reshape(16 * COEF, NY), up)
    b = exchange(to_b, "wide", 1)
    a = exchange(to_a, "wide", 0)
    tables, parents = make_tables(translate_far, coarse)
    out, into = pack(b, a, packed, to_b, tables)
    pair = exchange(into, "narrow", 0)
    cross = exchange(out, "narrow", 1)
    part, sums = inner(out, into, pair, tables)
    fine, coarse_locals = outer(cross, tables, part, sums)
    return fine.reshape(COEF, 4, 4, NY), parents, coarse_locals


def solution(mesh):
    return jax.shard_map(
        shards,
        mesh=mesh,
        in_specs=(P(None, "wide", "narrow", None), P(), P()),
        out_specs=(
            P(None, "wide", "narrow", None),
            P(None, "wide", "narrow", None),
            P(None, "wide", "narrow", None),
        ),
        check_vma=False,
    )
```
